256 devices in a mesh: pair: 32 (over y, z), tm: 8 (over x, core).
Axes of the slice: x: 4, y: 4, z: 8, core: 2. Of those that a mesh axis runs over, the one named last changes fastest.
Arguments:
- spectra: bfloat16 [4096, 16, 2, 4096], P('pair', 'tm'), may hold values from -6 to 6
- send_rows: int32 [32, 32, 4], P('pair'), may hold values from 0 to 127
- pair_list: int32 [2, 12288], P(None, 'pair'), may hold values from 0 to 127
- pair_count: int32 [32], P('pair'), may hold values from 128 to 384, as said below
Outputs:
- correlations: float32 [12288, 1024], P(('pair', 'tm'))
The draws below stay inside these ranges and needn't reach their ends.
Inputs may be any that keep to these rules, and one draw needn't show every extreme that they name: `pair_list`: indices into one owner's 32 * 4 received rows. `pair_count`: some owner has all 384 slots live; slots at and after the count are empty.
All inputs are finite; a program needn't handle non-finite values.
Results may differ from the reference program's by a relative error of at most 0.0003.
Values may be sent and summed in bfloat16 or wider, within the bound.
A program may use at most 192 MiB of HBM per device.

```python
import math
import jax
import jax.numpy as jnp
from jax import lax

F = 4096
LAGS = 1024
BLK = 128
CAP = 4
PAIRS_DEV = 384
OWNERS = 32
CHANNELS = 4096
WINDOWS = 16
PAIRS = 12288


def draw_pair_count(key, part):
    key = jax.random.fold_in(key, 7)
    key_counts, key_full = jax.random.split(key)
    counts = jax.random.randint(key_counts, (OWNERS,), PAIRS_DEV // 3, PAIRS_DEV + 1)
    full_owner = jax.random.randint(key_full, (), 0, OWNERS)
    return jnp.where(jnp.arange(OWNERS) == full_owner, PAIRS_DEV, counts).astype(jnp.int32)


def touch_ends(array, own_key, low, largest):
    place = [jax.random.randint(jax.random.fold_in(own_key, axis), (), 0, length) for axis, length in enumerate(array.shape)]
    widest = array.shape.index(max(array.shape))
    neighbour = place[:widest] + [(place[widest] + 1) % array.shape[widest]] + place[widest + 1:]
    return array.at[tuple(place)].set(low).at[tuple(neighbour)].set(largest)


def steps_of(own_key, shape, cuts, least, largest):
    gain = 1.0
    for position, shards_of in cuts:
        draws = jax.random.uniform(jax.random.fold_in(jax.random.fold_in(own_key, 6), position), (shards_of,), jnp.float32, least / len(cuts), largest / len(cuts))
        gain = gain * jnp.repeat(jnp.exp(draws), shape[position] // shards_of).reshape((-1,) + (1,) * (len(shape) - 1 - position))
    return gain


def noise(key, shape, deviation, bound, cuts=(), kind=jnp.bfloat16):
    loudness = steps_of(key, shape, cuts, -0.22, 0.18) if cuts else 1.0
    entries = jax.random.normal(key, shape, jnp.float32) * deviation * loudness
    return jnp.minimum(jnp.maximum(entries, -bound), bound).astype(kind)


def setup_inputs(seed: int = 0) -> dict:
    key_list = jax.random.split(jax.random.key(seed), 5)
    spectra = noise(key_list[0], (CHANNELS, WINDOWS, 2, F), 1.0, 6.0, ((0, 32), (1, 8)))
    send_rows = touch_ends(jax.random.randint(key_list[1], (OWNERS, OWNERS, CAP), 0, BLK), jax.random.fold_in(key_list[1], 1), 0, BLK - 1).astype(jnp.int32)
    pair_list = touch_ends(jax.random.randint(key_list[2], (2, PAIRS), 0, OWNERS * CAP), jax.random.fold_in(key_list[2], 1), 0, (OWNERS * CAP) - 1).astype(jnp.int32)
    pair_count = draw_pair_count(jax.random.fold_in(key_list[4], 71), 0)
    return {"spectra": spectra, "send_rows": send_rows, "pair_list": pair_list, "pair_count": pair_count}


def phase_tables(bins, lags):
    freq = jnp.arange(bins, dtype=jnp.int32)
    delay = jnp.arange(lags, dtype=jnp.int32) - lags // 2
    turns = (freq[:, None] * delay[None, :]) % (2 * bins)
    angle = turns.astype(jnp.float32) * (math.pi / bins)
    return jnp.cos(angle), jnp.sin(angle)


def reference(spectra, send_rows, pair_list, pair_count):
    cosine, sine = phase_tables(F, LAGS)
    scale = (2.0 * F * WINDOWS) ** -0.5
    senders = jnp.arange(OWNERS, dtype=jnp.int32)

    def one_owner(owner):
        routed = (senders[:, None] * BLK + send_rows[:, owner, :]).reshape(-1)
        left_ids = lax.dynamic_slice_in_dim(pair_list[0], owner * PAIRS_DEV, PAIRS_DEV, 0)
        right_ids = lax.dynamic_slice_in_dim(pair_list[1], owner * PAIRS_DEV, PAIRS_DEV, 0)
        left_rows = spectra[routed[left_ids]].astype(jnp.float32)
        right_rows = spectra[routed[right_ids]].astype(jnp.float32)
        real_part = jnp.sum(left_rows[:, :, 0] * right_rows[:, :, 0] + left_rows[:, :, 1] * right_rows[:, :, 1], axis=1)
        imag_part = jnp.sum(left_rows[:, :, 1] * right_rows[:, :, 0] - left_rows[:, :, 0] * right_rows[:, :, 1], axis=1)
        active = (jnp.arange(PAIRS_DEV, dtype=jnp.int32) < pair_count[owner]).astype(jnp.float32)[:, None]
        real_part = real_part * active
        imag_part = imag_part * active
        lagged = jnp.dot(real_part, cosine, precision=lax.Precision.HIGHEST) - jnp.dot(imag_part, sine, precision=lax.Precision.HIGHEST)
        return lagged * scale

    result = lax.map(one_owner, jnp.arange(OWNERS, dtype=jnp.int32))
    return result.reshape(OWNERS * PAIRS_DEV, LAGS)
```

```python
import functools
import math

import jax
import jax.numpy as jnp
import ml_dtypes
import numpy as np
from jax import lax
from jax.experimental import pallas as pl
from jax.experimental.pallas import tpu as pltpu
from jax.sharding import PartitionSpec as P

MESH = pl.DeviceIdType.MESH
LAGS = 1024
LANES = 128
GROUP = 8
F32 = jnp.float32
BF16 = jnp.bfloat16


def lag_table(bins, lags):
    freq = np.arange(bins, dtype=np.int64)
    delay = np.arange(lags, dtype=np.int64) - lags // 2
    angle = (freq[:, None] * delay[None, :] % (2 * bins)).astype(np.float64) * (math.pi / bins)
    both = np.stack([np.cos(angle), -np.sin(angle)]).astype(np.float32)
    both = both.reshape(2, bins // LANES, LANES, lags).transpose(1, 0, 2, 3).reshape(bins // LANES, 2 * LANES, lags)
    high = both.astype(ml_dtypes.bfloat16)
    low = (both - high.astype(np.float32)).astype(ml_dtypes.bfloat16)
    return np.stack([high, low], axis=1)


def kernel(dims, x_hbm, rows_ref, pairs_ref, count_ref, table_hbm, out_ref,
           *scratch):
    owners, times, capacity, windows, groups, npairs, chunks, scale = dims
    xbufs, scratch = scratch[:groups], scratch[groups:]
    stage, sendbuf, recvbuf, ohot, dhi, dlo, tbuf, acc, summed, xsem, tsem, ssem, rsem, lsem, psem, qsem = scratch
    me = lax.axis_index("pair")
    tm = lax.axis_index("tm")
    share = npairs // times

    def load_x(g, w):
        rows = pl.ds((w * groups + g) * 2 * GROUP, 2 * GROUP)
        to = pl.ds(w * 2 * GROUP, 2 * GROUP)
        return pltpu.make_async_copy(x_hbm.at[:, rows, :], xbufs[g].at[:, to, :], xsem.at[g, w])

    def load_table(g):
        return pltpu.make_async_copy(table_hbm.at[pl.ds(g * GROUP, GROUP)], tbuf.at[g % 2], tsem.at[g])

    for w in range(windows):
        load_x(0, w).start()

    barrier = pltpu.get_barrier_semaphore()

    def greet_owner(i, _):
        pl.semaphore_signal(barrier, inc=1, device_id=(lax.rem(me + i, owners), tm), device_id_type=MESH)
        return 0

    def greet_time(i, _):
        pl.semaphore_signal(barrier, inc=1, device_id=(me, lax.rem(tm + i, times)), device_id_type=MESH)
        return 0

    lax.fori_loop(1, owners, greet_owner, 0)
    lax.fori_loop(1, times, greet_time, 0)
    for g in range(1, groups):
        for w in range(windows):
            load_x(g, w).start()
    load_table(0).start()
    load_table(1).start()

    def prepare(g):
        for w in range(windows):
            load_x(g, w).wait()

        def one(o, _):
            base = lax.rem(o, 4) * (16 * GROUP)
            for k in range(capacity):
                r = rows_ref[k, o]
                for w in range(windows):
                    v = xbufs[g][r, w * 2 * GROUP : (w + 1) * 2 * GROUP, :]
                    stage[pl.ds(base + k * windows + w, 2 * GROUP, stride=8), :] = v.astype(F32)
            for t in range(GROUP):
                sendbuf[g, o, :, t * LANES : (t + 1) * LANES] = stage[pl.ds(base + t * 16, 16), :].astype(BF16)
            return 0

        lax.fori_loop(0, owners, one, 0, unroll=2)

    def lanes(c):
        g, t0, nt = chunks[c]
        return pl.ds(t0 * LANES, nt * LANES)

    def send(c):
        g = chunks[c][0]

        def one(i, _):
            to = lax.rem(me + i, owners)
            pltpu.make_async_remote_copy(
                src_ref=sendbuf.at[g, to, :, lanes(c)], dst_ref=recvbuf.at[g, me, :, lanes(c)],
                send_sem=ssem.at[c], recv_sem=rsem.at[c], device_id=(to, tm), device_id_type=MESH,
            ).start()
            return 0

        lax.fori_loop(1, owners, one, 0)
        pltpu.make_async_copy(sendbuf.at[g, me, :, lanes(c)], recvbuf.at[g, me, :, lanes(c)], lsem.at[c]).start()

    def wait_received(c):
        g = chunks[c][0]
        others = recvbuf.at[g, pl.ds(0, owners - 1), :, lanes(c)]
        pltpu.make_async_copy(others, others, rsem.at[c]).wait()
        own = recvbuf.at[g, me, :, lanes(c)]
        pltpu.make_async_copy(own, own, lsem.at[c]).wait()

    def wait_sent(c):
        g = chunks[c][0]
        others = sendbuf.at[g, pl.ds(0, owners - 1), :, lanes(c)]
        pltpu.make_async_copy(others, others, ssem.at[c]).wait()

    for g in range(groups):
        prepare(g)
        if g == 0:
            pl.semaphore_wait(barrier, owners - 1 + times - 1)
        for c in range(len(chunks)):
            if chunks[c][0] == g:
                send(c)

    column = lax.broadcasted_iota(jnp.int32, (npairs, 16 * owners), 1)
    slot = lax.broadcasted_iota(jnp.int32, (npairs, 16 * owners), 0)
    live = slot < count_ref[0]
    for side in range(2):
        ids = jnp.transpose(jnp.broadcast_to(pairs_ref[side : side + 1, :], (LANES, npairs)))
        line = (ids // capacity) * 16 + lax.rem(ids, capacity) * windows
        line = jnp.concatenate([line] * (16 * owners // LANES), axis=1)
        for part in range(2):
            for w in range(windows):
                hit = column == line + (part * 8 + w)
                if side == 0:
                    hit = hit & live
                ohot[side, part, w] = jnp.where(hit, 1.0, 0.0).astype(F32).astype(BF16)

    acc[...] = jnp.zeros(acc.shape, F32)

    def products(g, t0, first):
        at = pl.multiple_of(t0 * LANES, 2 * LANES)
        rows = recvbuf[g, :, :, pl.ds(at, 2 * LANES)].reshape(16 * owners, 2 * LANES)
        real = None
        for w in range(windows):
            a = [jnp.dot(ohot[0, part, w], rows, preferred_element_type=F32) for part in range(2)]
            b = [jnp.dot(ohot[1, part, w], rows, preferred_element_type=F32) for part in range(2)]
            re = a[0] * b[0] + a[1] * b[1]
            im = a[1] * b[0] - a[0] * b[1]
            real, imag = (re, im) if real is None else (real + re, imag + im)
        for i, value in enumerate((real, imag)):
            high = value.astype(BF16)
            low = (value - high.astype(F32)).astype(BF16)
            for t in range(2):
                to = pl.ds(pl.multiple_of((t0 - first + t) * 2 * LANES, 2 * LANES) + i * LANES, LANES)
                dhi[:, to] = high[:, t * LANES : (t + 1) * LANES]
                dlo[:, to] = low[:, t * LANES : (t + 1) * LANES]

    for c, (g, t0, nt) in enumerate(chunks):
        wait_received(c)

        def piece(i, _):
            products(g, t0 + 2 * i, t0)
            return 0

        lax.fori_loop(0, nt // 2, piece, 0)
        if t0 == 0:
            load_table(g).wait()
        depth = nt * 2 * LANES

        def lag_tile(n, _):
            at = pl.ds(pl.multiple_of(n * 256, 256), 256)
            thi = tbuf[g % 2, t0 : t0 + nt, 0, :, at].reshape(depth, 256)
            tlo = tbuf[g % 2, t0 : t0 + nt, 1, :, at].reshape(depth, 256)
            high = dhi[:, :depth]
            total = jnp.dot(high, thi, preferred_element_type=F32)
            total += jnp.dot(dlo[:, :depth], thi, preferred_element_type=F32)
            total += jnp.dot(high, tlo, preferred_element_type=F32)
            acc[:, at] += total
            return 0

        lax.fori_loop(0, LAGS // 256, lag_tile, 0)
        if t0 + nt == GROUP and g + 2 < groups:
            load_table(g + 2).start()

    def give(i, _):
        to = lax.rem(tm + i, times)
        pltpu.make_async_remote_copy(
            src_ref=acc.at[pl.ds(to * share, share), :], dst_ref=summed.at[tm],
            send_sem=psem, recv_sem=qsem, device_id=(me, to), device_id_type=MESH,
        ).start()
        return 0

    lax.fori_loop(1, times, give, 0)
    summed[tm] = acc[pl.ds(pl.multiple_of(tm * share, 8), share), :]
    received = summed.at[pl.ds(0, times - 1)]
    pltpu.make_async_copy(received, received, qsem).wait()
    total = summed[0]
    for t in range(1, times):
        total = total + summed[t]
    out_ref[...] = total * scale
    given = acc.at[pl.ds(0, (times - 1) * share), :]
    pltpu.make_async_copy(given, given, psem).wait()
    for c in range(len(chunks)):
        wait_sent(c)


def shards(table, spectra, send_rows, pair_list, pair_count):
    owners = lax.axis_size("pair")
    times = lax.axis_size("tm")
    channels, windows, _, bins = spectra.shape
    capacity = send_rows.shape[2]
    npairs = pair_list.shape[1]
    tiles = bins // LANES
    groups = tiles // GROUP
    lines = spectra.reshape(channels, windows, 2, tiles, LANES).transpose(0, 1, 3, 2, 4)
    lines = lines.reshape(channels, windows * tiles * 2, LANES)
    chunks = [(g, 0, GROUP) for g in range(groups - 1)]
    chunks += [(groups - 1, 0, 4), (groups - 1, 4, 2), (groups - 1, 6, 2)]
    scale = (2.0 * bins * windows * times) ** (-0.5)
    dims = (owners, times, capacity, windows, groups, npairs, tuple(chunks), scale)
    rows = jnp.transpose(send_rows, (0, 2, 1)).reshape(capacity, owners)
    count = len(chunks)
    dma = pltpu.SemaphoreType.DMA
    return pl.pallas_call(
        functools.partial(kernel, dims),
        out_shape=jax.ShapeDtypeStruct((npairs // times, LAGS), F32),
        in_specs=[
            pl.BlockSpec(memory_space=pl.ANY),
            pl.BlockSpec(memory_space=pltpu.SMEM),
            pl.BlockSpec(memory_space=pltpu.VMEM),
            pl.BlockSpec(memory_space=pltpu.SMEM),
            pl.BlockSpec(memory_space=pl.ANY),
        ],
        out_specs=pl.BlockSpec(memory_space=pltpu.VMEM),
        scratch_shapes=[
            *[pltpu.VMEM((channels, windows * 2 * GROUP, LANES), BF16)] * groups,
            pltpu.VMEM((4 * 16 * GROUP, LANES), F32),
            pltpu.VMEM((groups, owners, 16, GROUP * LANES), BF16),
            pltpu.VMEM((groups, owners, 16, GROUP * LANES), BF16),
            pltpu.VMEM((2, 2, windows, npairs, 16 * owners), BF16),
            pltpu.VMEM((npairs, GROUP * 2 * LANES), BF16),
            pltpu.VMEM((npairs, GROUP * 2 * LANES), BF16),
            pltpu.VMEM((2, GROUP, 2, 2 * LANES, LAGS), BF16),
            pltpu.VMEM((npairs, LAGS), F32),
            pltpu.VMEM((times, npairs // times, LAGS), F32),
            dma((groups, windows)),
            dma((groups,)),
            dma((count,)),
            dma((count,)),
            dma((count,)),
            dma,
            dma,
        ],
        compiler_params=pltpu.CompilerParams(
            collective_id=0, has_side_effects=True, vmem_limit_bytes=56 * 1024 * 1024
        ),
        name="correlate",
    )(lines, rows, pair_list, pair_count, table)


def solution(mesh):
    table = lag_table(4096, LAGS)

    def run(spectra, send_rows, pair_list, pair_count):
        in_specs = (P(), P("pair", "tm", None, None), P("pair", None, None), P(None, "pair"), P("pair"))
        body = jax.shard_map(
            shards, mesh=mesh, in_specs=in_specs, out_specs=P(("pair", "tm"), None), check_vma=False
        )
        return body(jnp.asarray(table), spectra, send_rows, pair_list, pair_count)

    return run
```

```python
import functools
import math

import jax
import jax.numpy as jnp
import numpy as np
from jax import lax
from jax.experimental import pallas as pl
from jax.experimental.pallas import tpu as pltpu
from jax.sharding import PartitionSpec as P

MESH = pl.DeviceIdType.MESH
LAGS = 1024
LANES = 128
GROUP = 8
F32 = jnp.float32
BF16 = jnp.bfloat16


def lag_tables(bins, lags):
    delay = np.arange(lags, dtype=np.int64) - lags // 2

    def pair(freq):
        angle = (freq[:, None] * delay[None, :] % (2 * bins)).astype(np.float64) * (math.pi / bins)
        return np.cos(angle).astype(np.float32), np.sin(angle).astype(np.float32)

    first = np.stack(pair(np.arange(bins // LANES, dtype=np.int64) * LANES), axis=1)
    added = np.stack(pair(np.arange(LANES, dtype=np.int64)))
    return first, added


def kernel(dims, x_hbm, rows_hbm, pairs_hbm, count_hbm, first_hbm, added_hbm, out_ref,
           *scratch):
    owners, times, capacity, windows, groups, npairs, chunks, scale = dims
    xbufs, scratch = scratch[:groups], scratch[groups:]
    rows_ref, pairs_ref, count_ref, stage, sendbuf, latebuf, recvbuf, ohot, scratch = *scratch[:8], scratch[8:]
    dhi, dlo, tbuf, first, added, acc, summed, stack, parts, scratch = *scratch[:9], scratch[9:]
    xsem, tsem, ssem, rsem, lsem, esem, psem, qsem, usem, vsem = scratch
    late = groups - 1
    me = lax.axis_index("pair")
    tm = lax.axis_index("tm")
    share = npairs // times

    def load_x(g, w):
        rows = pl.ds((w * groups + g) * 2 * GROUP, 2 * GROUP)
        to = pl.ds(w * 2 * GROUP, 2 * GROUP)
        return pltpu.make_async_copy(x_hbm.at[:, rows, :], xbufs[g].at[:, to, :], xsem.at[g, w])

    def load_tables():
        return [
            pltpu.make_async_copy(pairs_hbm, pairs_ref, tsem.at[0]),
            pltpu.make_async_copy(count_hbm, count_ref, tsem.at[1]),
            pltpu.make_async_copy(first_hbm, first, tsem.at[2]),
            pltpu.make_async_copy(added_hbm, added, tsem.at[3]),
        ]

    rows_copy = pltpu.make_async_copy(rows_hbm, rows_ref, tsem.at[4])
    rows_copy.start()
    for w in range(windows):
        load_x(0, w).start()

    barrier = pltpu.get_barrier_semaphore()

    def greet_owner(i, _):
        pl.semaphore_signal(barrier, inc=1, device_id=(lax.rem(me + i, owners), tm), device_id_type=MESH)
        return 0

    def greet_time(i, _):
        pl.semaphore_signal(barrier, inc=1, device_id=(me, lax.rem(tm + i, times)), device_id_type=MESH)
        return 0

    lax.fori_loop(1, owners, greet_owner, 0)
    lax.fori_loop(1, times, greet_time, 0)
    for g in range(1, groups):
        for w in range(windows):
            load_x(g, w).start()
    for copy in load_tables():
        copy.start()

    rows_copy.wait()

    def prepare(g):
        for w in range(windows):
            load_x(g, w).wait()

        def one(o, _):
            base = lax.rem(o, 4) * (16 * GROUP)
            for k in range(capacity):
                r = rows_ref[k, o]
                for w in range(windows):
                    v = xbufs[g][r, w * 2 * GROUP : (w + 1) * 2 * GROUP, :]
                    stage[pl.ds(base + k * windows + w, 2 * GROUP, stride=8), :] = v.astype(F32)
            for t in range(GROUP):
                sendbuf[g, o, :, t * LANES : (t + 1) * LANES] = stage[pl.ds(base + t * 16, 16), :].astype(BF16)
            return 0

        lax.fori_loop(0, owners, one, 0, unroll=2)

    def lanes(c):
        g, t0, nt = chunks[c]
        return pl.ds(t0 * LANES, nt * LANES)

    def source(g):
        return latebuf if g == late else sendbuf.at[g]

    def send(c):
        g = chunks[c][0]

        def one(i, _):
            to = lax.rem(me + i, owners)
            pltpu.make_async_remote_copy(
                src_ref=source(g).at[to, :, lanes(c)], dst_ref=recvbuf.at[g, me, :, lanes(c)],
                send_sem=ssem.at[c], recv_sem=rsem.at[c], device_id=(to, tm), device_id_type=MESH,
            ).start()
            return 0

        lax.fori_loop(1, owners, one, 0)
        pltpu.make_async_copy(source(g).at[me, :, lanes(c)], recvbuf.at[g, me, :, lanes(c)], lsem.at[c]).start()

    def wait_received(c):
        g = chunks[c][0]
        others = recvbuf.at[g, pl.ds(0, owners - 1), :, lanes(c)]
        pltpu.make_async_copy(others, others, rsem.at[c]).wait()
        own = recvbuf.at[g, me, :, lanes(c)]
        pltpu.make_async_copy(own, own, lsem.at[c]).wait()

    def wait_sent(c):
        g = chunks[c][0]
        others = source(g).at[pl.ds(0, owners - 1), :, lanes(c)]
        pltpu.make_async_copy(others, others, ssem.at[c]).wait()

    def tile(t):
        return pl.ds(pl.multiple_of(t * LANES, LANES), LANES)

    own_tile = pltpu.make_async_copy(sendbuf.at[late, :, :, tile(tm)], latebuf.at[:, :, tile(tm)], esem.at[2])

    def trade():
        def one(i, _):
            to = lax.rem(tm + i, times)
            pltpu.make_async_remote_copy(
                src_ref=sendbuf.at[late, :, :, tile(to)], dst_ref=latebuf.at[:, :, tile(tm)],
                send_sem=esem.at[0], recv_sem=esem.at[1], device_id=(me, to), device_id_type=MESH,
            ).start()
            return 0

        lax.fori_loop(1, times, one, 0)
        own_tile.start()

    def wait_traded():
        others = latebuf.at[:, :, pl.ds(0, (times - 1) * LANES)]
        pltpu.make_async_copy(others, others, esem.at[1]).wait()
        own_tile.wait()

    for g in (0, late, *range(1, late)):
        prepare(g)
        if g == 0:
            pl.semaphore_wait(barrier, owners - 1 + times - 1)
        if g == late:
            trade()
        for c in range(len(chunks)):
            if chunks[c][0] == g < late:
                send(c)

    for copy in load_tables():
        copy.wait()

    column = lax.broadcasted_iota(jnp.int32, (npairs, 16 * owners), 1)
    slot = lax.broadcasted_iota(jnp.int32, (npairs, 16 * owners), 0)
    live = slot < count_ref[0]
    for side in range(2):
        ids = jnp.transpose(jnp.broadcast_to(pairs_ref[side : side + 1, :], (LANES, npairs)))
        line = (ids // capacity) * 16 + lax.rem(ids, capacity) * windows
        line = jnp.concatenate([line] * (16 * owners // LANES), axis=1)
        for part in range(2):
            for w in range(windows):
                hit = column == line + (part * 8 + w)
                if side == 0:
                    hit = hit & live
                ohot[side, part, w] = jnp.where(hit, 1.0, 0.0).astype(F32).astype(BF16)

    acc[...] = jnp.zeros(acc.shape, F32)

    def split(value):
        high = value.astype(BF16)
        return high, (value - high.astype(F32)).astype(BF16)

    def make_table(g):
        def one(i, _):
            t, n = i // (LAGS // 256), lax.rem(i, LAGS // 256)
            at = pl.ds(pl.multiple_of(n * 256, 256), 256)
            c0, s0 = first[g * GROUP + t, 0:1, at], first[g * GROUP + t, 1:2, at]
            c1, s1 = added[0, :, at], added[1, :, at]
            for row, value in ((0, c0 * c1 - s0 * s1), (LANES, -(s0 * c1 + c0 * s1))):
                high, low = split(value)
                tbuf[t, 0, row : row + LANES, at] = high
                tbuf[t, 1, row : row + LANES, at] = low
            return 0

        lax.fori_loop(0, GROUP * (LAGS // 256), one, 0)

    def cross(g, at, width):
        rows = recvbuf[g, :, :, pl.ds(at, width)].reshape(16 * owners, width)
        real = None
        for w in range(windows):
            a = [jnp.dot(ohot[0, part, w], rows, preferred_element_type=F32) for part in range(2)]
            b = [jnp.dot(ohot[1, part, w], rows, preferred_element_type=F32) for part in range(2)]
            re = a[0] * b[0] + a[1] * b[1]
            im = a[1] * b[0] - a[0] * b[1]
            real, imag = (re, im) if real is None else (real + re, imag + im)
        return real, imag

    def early_chunk(g, t0, nt):
        def piece(i, _):
            at = pl.multiple_of((t0 + 2 * i) * LANES, 2 * LANES)
            for part, value in enumerate(cross(g, at, 2 * LANES)):
                high, low = split(value)
                for t in range(2):
                    to = pl.ds(pl.multiple_of((2 * i + t) * 2 * LANES, 2 * LANES) + part * LANES, LANES)
                    dhi[:, to] = high[:, t * LANES : (t + 1) * LANES]
                    dlo[:, to] = low[:, t * LANES : (t + 1) * LANES]
            return 0

        lax.fori_loop(0, nt // 2, piece, 0)
        depth = nt * 2 * LANES

        def lag_tile(n, _):
            at = pl.ds(pl.multiple_of(n * 256, 256), 256)
            thi = tbuf[t0 : t0 + nt, 0, :, at].reshape(depth, 256)
            tlo = tbuf[t0 : t0 + nt, 1, :, at].reshape(depth, 256)
            high = dhi[:, :depth]
            total = jnp.dot(high, thi, preferred_element_type=F32)
            total += jnp.dot(dlo[:, :depth], thi, preferred_element_type=F32)
            total += jnp.dot(high, tlo, preferred_element_type=F32)
            acc[:, at] += total
            return 0

        lax.fori_loop(0, LAGS // 256, lag_tile, 0)

    def late_chunk(t0, nt):
        def piece(i, _):
            at = pl.multiple_of((t0 + 2 * i) * LANES, 2 * LANES)
            for part, value in enumerate(cross(late, at, 2 * LANES)):
                stack[:, part * LANES : (part + 1) * LANES] += value[:, :LANES] + value[:, LANES:]
            return 0

        if nt > 1:
            lax.fori_loop(0, nt // 2, piece, 0)
        else:
            for part, value in enumerate(cross(late, t0 * LANES, LANES)):
                stack[:, part * LANES : (part + 1) * LANES] += value

    def block(t):
        return pl.ds(pl.multiple_of(t * share, 8), share)

    def give(src, dst, send_sem, recv_sem):
        def one(i, _):
            to = lax.rem(tm + i, times)
            pltpu.make_async_remote_copy(
                src_ref=src.at[block(to), :], dst_ref=dst.at[tm], send_sem=send_sem, recv_sem=recv_sem.at[i],
                device_id=(me, to), device_id_type=MESH,
            ).start()
            return 0

        lax.fori_loop(1, times, one, 0)

    def wait_given(src, sem):
        given = src.at[pl.ds(0, (times - 1) * share), :]
        pltpu.make_async_copy(given, given, sem).wait()

    def wait_part(dst, sem, i):
        come = dst.at[lax.rem(tm + times - i, times)]
        pltpu.make_async_copy(come, come, sem.at[i]).wait()

    stack[...] = jnp.zeros(stack.shape, F32)
    for c, (g, t0, nt) in enumerate(chunks):
        if t0 == 0:
            make_table(g)
        if c == 1:
            wait_traded()
            for d in range(len(chunks)):
                if chunks[d][0] == late:
                    send(d)
        wait_received(c)
        if g < late:
            early_chunk(g, t0, nt)
        else:
            late_chunk(t0, nt)
        if g < late and chunks[c + 1][0] == late:
            give(acc, summed, psem, qsem)

    give(stack, parts, usem, vsem)
    for i in range(1, times):
        wait_part(summed, qsem, i)
    summed[tm] = acc[block(tm), :]
    total = summed[0]
    for t in range(1, times):
        total = total + summed[t]
    out_ref[...] = total * scale
    parts[tm] = stack[block(tm), :]

    def lag_part(j, _):
        odd = lax.rem(j, 2)
        i = odd * ((j + 1) // 2) + (1 - odd) * (lax.rem(times - j // 2, times))

        @pl.when(j > 0)
        def _():
            wait_part(parts, vsem, i)

        t = lax.rem(tm + times - i, times)
        high, low = split(parts[t])
        thi, tlo = tbuf[t, 0], tbuf[t, 1]
        value = jnp.dot(jnp.concatenate([high, low]), thi, preferred_element_type=F32)
        value = value[:share] + value[share:] + jnp.dot(high, tlo, preferred_element_type=F32)
        out_ref[...] += value * scale
        return 0

    lax.fori_loop(0, times, lag_part, 0)
    wait_given(acc, psem)
    wait_given(stack, usem)
    others = sendbuf.at[late, :, :, pl.ds(0, (times - 1) * LANES)]
    pltpu.make_async_copy(others, others, esem.at[0]).wait()
    for c in range(len(chunks)):
        wait_sent(c)


def shards(first, added, spectra, send_rows, pair_list, pair_count):
    owners = lax.axis_size("pair")
    times = lax.axis_size("tm")
    channels, windows, _, bins = spectra.shape
    capacity = send_rows.shape[2]
    npairs = pair_list.shape[1]
    tiles = bins // LANES
    groups = tiles // GROUP
    lines = spectra.reshape(channels, windows, 2, tiles, LANES).transpose(0, 1, 3, 2, 4)
    lines = lines.reshape(channels, windows * tiles * 2, LANES)
    last = groups - 1
    chunks = [(g, 0, GROUP) for g in range(last - 1)]
    chunks += [(last - 1, 0, 4), (last - 1, 4, 2), (last - 1, 6, 2)]
    chunks += [(last, 0, 4), (last, 4, 2), (last, 6, 1), (last, 7, 1)]
    scale = (2.0 * bins * windows * times) ** (-0.5)
    dims = (owners, times, capacity, windows, groups, npairs, tuple(chunks), scale)
    rows = jnp.transpose(send_rows, (0, 2, 1)).reshape(capacity, owners)
    nc = len(chunks)
    dma = pltpu.SemaphoreType.DMA
    return pl.pallas_call(
        functools.partial(kernel, dims),
        out_shape=pltpu.VMEM((npairs // times, LAGS), F32),
        in_specs=[pl.BlockSpec(memory_space=pltpu.HBM)] * 6,
        out_specs=pl.BlockSpec(memory_space=pltpu.VMEM),
        scratch_shapes=[
            *[pltpu.VMEM((channels, windows * 2 * GROUP, LANES), BF16)] * groups,
            pltpu.SMEM(rows.shape, jnp.int32),
            pltpu.VMEM(pair_list.shape, jnp.int32),
            pltpu.SMEM((1,), jnp.int32),
            pltpu.VMEM((4 * 16 * GROUP, LANES), F32),
            pltpu.VMEM((groups, owners, 16, GROUP * LANES), BF16),
            pltpu.VMEM((owners, 16, GROUP * LANES), BF16),
            pltpu.VMEM((groups, owners, 16, GROUP * LANES), BF16),
            pltpu.VMEM((2, 2, windows, npairs, 16 * owners), BF16),
            pltpu.VMEM((npairs, GROUP * 2 * LANES), BF16),
            pltpu.VMEM((npairs, GROUP * 2 * LANES), BF16),
            pltpu.VMEM((GROUP, 2, 2 * LANES, LAGS), BF16),
            pltpu.VMEM(first.shape, F32),
            pltpu.VMEM(added.shape, F32),
            pltpu.VMEM((npairs, LAGS), F32),
            pltpu.VMEM((times, npairs // times, LAGS), F32),
            pltpu.VMEM((npairs, 2 * LANES), F32),
            pltpu.VMEM((times, npairs // times, 2 * LANES), F32),
            dma((groups, windows)),
            dma((5,)),
            dma((nc,)),
            dma((nc,)),
            dma((nc,)),
            dma((3,)),
            dma,
            dma((times,)),
            dma,
            dma((times,)),
        ],
        compiler_params=pltpu.CompilerParams(
            collective_id=0, has_side_effects=True, vmem_limit_bytes=58 * 1024 * 1024
        ),
        name="correlate",
    )(lines, rows, pair_list, pair_count, first, added)


def solution(mesh):
    first, added = lag_tables(4096, LAGS)

    def run(spectra, send_rows, pair_list, pair_count):
        in_specs = (P(), P(), P("pair", "tm", None, None), P("pair", None, None), P(None, "pair"), P("pair"))
        body = jax.shard_map(
            shards, mesh=mesh, in_specs=in_specs, out_specs=P(("pair", "tm"), None), check_vma=False
        )
        return body(jnp.asarray(first), jnp.asarray(added), spectra, send_rows, pair_list, pair_count)

    return run
```

```python
import functools
import math

import jax
import jax.numpy as jnp
import numpy as np
from jax import lax
from jax.experimental import pallas as pl
from jax.experimental.pallas import tpu as pltpu
from jax.sharding import PartitionSpec as P

MESH = pl.DeviceIdType.MESH
LAGS = 1024
LANES = 128
HALF = LANES // 2
GROUP = 8
F32 = jnp.float32
BF16 = jnp.bfloat16


def lag_tables(bins, lags):
    delay = np.arange(lags, dtype=np.int64) - lags // 2

    def pair(freq):
        angle = (freq[:, None] * delay[None, :] % (2 * bins)).astype(np.float64) * (math.pi / bins)
        return np.cos(angle).astype(np.float32), np.sin(angle).astype(np.float32)

    first = np.stack(pair(np.arange(bins // LANES, dtype=np.int64) * LANES), axis=1)
    added = np.stack(pair(np.arange(LANES, dtype=np.int64)))
    return first, added


def kernel(dims, x_hbm, rows_hbm, pairs_hbm, count_hbm, first_hbm, added_hbm, out_ref,
           *scratch):
    owners, times, capacity, windows, groups, npairs, chunks, scale = dims
    xbufs, scratch = scratch[:groups], scratch[groups:]
    rows_ref, pairs_ref, count_ref, stage, sendbuf, latebuf, recvbuf, ohot, scratch = *scratch[:8], scratch[8:]
    dhi, dlo, tbuf, first, added, acc, summed, sums, stack, parts, packed, scratch = *scratch[:11], scratch[11:]
    xsem, tsem, ssem, rsem, lsem, esem, psem, qsem, usem, vsem = scratch
    late = groups - 1
    me = lax.axis_index("pair")
    tm = lax.axis_index("tm")
    share = npairs // times

    def load_x(g, w):
        rows = pl.ds((w * groups + g) * 2 * GROUP, 2 * GROUP)
        to = pl.ds(w * 2 * GROUP, 2 * GROUP)
        return pltpu.make_async_copy(x_hbm.at[:, rows, :], xbufs[g].at[:, to, :], xsem.at[g, w])

    def load_tables():
        return [
            pltpu.make_async_copy(pairs_hbm, pairs_ref, tsem.at[0]),
            pltpu.make_async_copy(count_hbm, count_ref, tsem.at[1]),
            pltpu.make_async_copy(first_hbm, first, tsem.at[2]),
            pltpu.make_async_copy(added_hbm, added, tsem.at[3]),
        ]

    rows_copy = pltpu.make_async_copy(rows_hbm, rows_ref, tsem.at[4])
    rows_copy.start()
    for w in range(windows):
        load_x(0, w).start()

    barrier = pltpu.get_barrier_semaphore()

    def greet_owner(i, _):
        pl.semaphore_signal(barrier, inc=1, device_id=(lax.rem(me + i, owners), tm), device_id_type=MESH)
        return 0

    def greet_time(i, _):
        pl.semaphore_signal(barrier, inc=1, device_id=(me, lax.rem(tm + i, times)), device_id_type=MESH)
        return 0

    lax.fori_loop(1, owners, greet_owner, 0)
    lax.fori_loop(1, times, greet_time, 0)
    for g in range(1, groups):
        for w in range(windows):
            load_x(g, w).start()
    for copy in load_tables():
        copy.start()

    rows_copy.wait()

    def prepare(g):
        for w in range(windows):
            load_x(g, w).wait()

        def one(o, _):
            base = lax.rem(o, 4) * (16 * GROUP)
            for k in range(capacity):
                r = rows_ref[k, o]
                for w in range(windows):
                    v = xbufs[g][r, w * 2 * GROUP : (w + 1) * 2 * GROUP, :]
                    stage[pl.ds(base + k * windows + w, 2 * GROUP, stride=8), :] = v.astype(F32)
            for t in range(GROUP):
                sendbuf[g, o, :, t * LANES : (t + 1) * LANES] = stage[pl.ds(base + t * 16, 16), :].astype(BF16)
            return 0

        lax.fori_loop(0, owners, one, 0, unroll=2)

    def lanes(c):
        g, t0, nt = chunks[c]
        return pl.ds(t0 * LANES, nt * LANES)

    def source(g):
        return latebuf if g == late else sendbuf.at[g]

    def send(c):
        g = chunks[c][0]

        def one(i, _):
            to = lax.rem(me + i, owners)
            pltpu.make_async_remote_copy(
                src_ref=source(g).at[to, :, lanes(c)], dst_ref=recvbuf.at[g, me, :, lanes(c)],
                send_sem=ssem.at[c], recv_sem=rsem.at[c], device_id=(to, tm), device_id_type=MESH,
            ).start()
            return 0

        lax.fori_loop(1, owners, one, 0)
        pltpu.make_async_copy(source(g).at[me, :, lanes(c)], recvbuf.at[g, me, :, lanes(c)], lsem.at[c]).start()

    def wait_received(c):
        g = chunks[c][0]
        others = recvbuf.at[g, pl.ds(0, owners - 1), :, lanes(c)]
        pltpu.make_async_copy(others, others, rsem.at[c]).wait()
        own = recvbuf.at[g, me, :, lanes(c)]
        pltpu.make_async_copy(own, own, lsem.at[c]).wait()

    def wait_sent(c):
        g = chunks[c][0]
        others = source(g).at[pl.ds(0, owners - 1), :, lanes(c)]
        pltpu.make_async_copy(others, others, ssem.at[c]).wait()

    def tile(t):
        return pl.ds(pl.multiple_of(t * LANES, LANES), LANES)

    own_tile = pltpu.make_async_copy(sendbuf.at[late, :, :, tile(tm)], latebuf.at[:, :, tile(tm)], esem.at[2])

    def trade():
        def one(i, _):
            to = lax.rem(tm + i, times)
            pltpu.make_async_remote_copy(
                src_ref=sendbuf.at[late, :, :, tile(to)], dst_ref=latebuf.at[:, :, tile(tm)],
                send_sem=esem.at[0], recv_sem=esem.at[1], device_id=(me, to), device_id_type=MESH,
            ).start()
            return 0

        lax.fori_loop(1, times, one, 0)
        own_tile.start()

    def wait_traded():
        others = latebuf.at[:, :, pl.ds(0, (times - 1) * LANES)]
        pltpu.make_async_copy(others, others, esem.at[1]).wait()
        own_tile.wait()

        def pack(o, _):
            for row in range(times // 2):
                x = latebuf[o, :, row * 2 * LANES : (row * 2 + 1) * LANES].astype(F32)
                y = latebuf[o, :, (row * 2 + 1) * LANES : (row * 2 + 2) * LANES].astype(F32)
                for h in range(2):
                    cut = slice(h * HALF, (h + 1) * HALF)
                    packed[h * (times // 2) + row] = jnp.concatenate([x[:, cut], y[:, cut]], axis=1).astype(BF16)
            for t in range(times):
                latebuf[o, :, t * LANES : (t + 1) * LANES] = packed[t]
            return 0

        lax.fori_loop(0, owners, pack, 0)

    for g in (0, late, *range(1, late)):
        prepare(g)
        if g == 0:
            pl.semaphore_wait(barrier, owners - 1 + times - 1)
        if g == late:
            trade()
        for c in range(len(chunks)):
            if chunks[c][0] == g < late:
                send(c)

    for copy in load_tables():
        copy.wait()

    lines = 8 * owners
    column = lax.broadcasted_iota(jnp.int32, (npairs, lines), 1)
    slot = lax.broadcasted_iota(jnp.int32, (npairs, lines), 0)
    live = slot < count_ref[0]
    for side in range(2):
        ids = jnp.transpose(jnp.broadcast_to(pairs_ref[side : side + 1, :], (LANES, npairs)))
        line = jnp.concatenate([ids * windows] * (lines // LANES), axis=1)
        for w in range(windows):
            hit = column == line + w
            if side == 0:
                hit = hit & live
            ohot[side, w] = jnp.where(hit, 1.0, 0.0).astype(F32).astype(BF16)

    acc[...] = jnp.zeros(acc.shape, F32)

    def split(value):
        high = value.astype(BF16)
        return high, (value - high.astype(F32)).astype(BF16)

    def make_table(g):
        def one(i, _):
            t, n = i // (LAGS // 256), lax.rem(i, LAGS // 256)
            at = pl.ds(pl.multiple_of(n * 256, 256), 256)
            c0, s0 = first[g * GROUP + t, 0:1, at], first[g * GROUP + t, 1:2, at]
            c1, s1 = added[0, :, at], added[1, :, at]
            for part, value in enumerate((c0 * c1 - s0 * s1, -(s0 * c1 + c0 * s1))):
                for i, piece in enumerate(split(value)):
                    if g == late:
                        for h in range(2):
                            row = h * LANES + part * HALF
                            tbuf[t, i, row : row + HALF, at] = piece[h * HALF : (h + 1) * HALF]
                    else:
                        tbuf[t, i, part * LANES : (part + 1) * LANES, at] = piece
            return 0

        lax.fori_loop(0, GROUP * (LAGS // 256), one, 0)

    def cross(g, at, width):
        both = recvbuf[g, :, :, pl.ds(at, width)].astype(F32)
        rows = [both[:, part * 8 : part * 8 + 8, :].reshape(8 * owners, width).astype(BF16) for part in range(2)]
        rows = jnp.concatenate(rows, axis=1)
        real = None
        for w in range(windows):
            a = jnp.dot(ohot[0, w], rows, preferred_element_type=F32)
            b = jnp.dot(ohot[1, w], rows, preferred_element_type=F32)
            a, b = [(v[:, :width], v[:, width:]) for v in (a, b)]
            re = a[0] * b[0] + a[1] * b[1]
            im = a[1] * b[0] - a[0] * b[1]
            real, imag = (re, im) if real is None else (real + re, imag + im)
        return real, imag

    def early_chunk(g, t0, nt):
        def piece(i, _):
            at = pl.multiple_of((t0 + 2 * i) * LANES, 2 * LANES)
            for part, value in enumerate(cross(g, at, 2 * LANES)):
                high, low = split(value)
                for t in range(2):
                    to = pl.ds(pl.multiple_of((2 * i + t) * 2 * LANES, 2 * LANES) + part * LANES, LANES)
                    dhi[:, to] = high[:, t * LANES : (t + 1) * LANES]
                    dlo[:, to] = low[:, t * LANES : (t + 1) * LANES]
            return 0

        lax.fori_loop(0, nt // 2, piece, 0)
        depth = nt * 2 * LANES

        def lag_tile(n, _):
            at = pl.ds(pl.multiple_of(n * 256, 256), 256)
            thi = tbuf[t0 : t0 + nt, 0, :, at].reshape(depth, 256)
            tlo = tbuf[t0 : t0 + nt, 1, :, at].reshape(depth, 256)
            high = dhi[:, :depth]
            total = jnp.dot(high, thi, preferred_element_type=F32)
            total += jnp.dot(dlo[:, :depth], thi, preferred_element_type=F32)
            total += jnp.dot(high, tlo, preferred_element_type=F32)
            acc[:, at] += total
            return 0

        lax.fori_loop(0, LAGS // 256, lag_tile, 0)

    def late_chunk(t0, nt):
        def piece(i, _):
            at = pl.multiple_of((t0 + 2 * i) * LANES, 2 * LANES)
            for part, value in enumerate(cross(late, at, 2 * LANES)):
                sums[part] += value[:, :LANES] + value[:, LANES:]
            return 0

        if t0 % (times // 2) == 0:
            sums[...] = jnp.zeros(sums.shape, F32)
        if nt > 1:
            lax.fori_loop(0, nt // 2, piece, 0)
        else:
            for part, value in enumerate(cross(late, t0 * LANES, LANES)):
                sums[part] += value

    def finish_half(h):
        halves = [sums[part, :, :HALF] + sums[part, :, HALF:] for part in range(2)]
        stack[h] = jnp.concatenate(halves, axis=1)
        give(stack.at[h], parts.at[h], usem.at[h], vsem.at[h])
        parts[h, tm] = stack[h, block(tm), :]

    def block(t):
        return pl.ds(pl.multiple_of(t * share, 8), share)

    def give(src, dst, send_sem, recv_sem):
        def one(i, _):
            far = lax.rem(i, 2) * (times // 2 + (i - 1) // 2) + (1 - lax.rem(i, 2)) * (times // 2 - i // 2)
            to = lax.rem(tm + far, times)
            pltpu.make_async_remote_copy(
                src_ref=src.at[block(to), :], dst_ref=dst.at[tm], send_sem=send_sem, recv_sem=recv_sem.at[far],
                device_id=(me, to), device_id_type=MESH,
            ).start()
            return 0

        lax.fori_loop(1, times, one, 0)

    def wait_given(src, sem):
        given = src.at[pl.ds(0, (times - 1) * share), :]
        pltpu.make_async_copy(given, given, sem).wait()

    def wait_part(dst, sem, i):
        come = dst.at[lax.rem(tm + times - i, times)]
        pltpu.make_async_copy(come, come, sem.at[i]).wait()

    for c, (g, t0, nt) in enumerate(chunks):
        if t0 == 0:
            make_table(g)
        if c == 1:
            wait_traded()
            for d in range(len(chunks)):
                if chunks[d][0] == late:
                    send(d)
        wait_received(c)
        if g < late:
            early_chunk(g, t0, nt)
            if chunks[c + 1][0] == late:
                give(acc, summed, psem, qsem)
        else:
            late_chunk(t0, nt)
            if (t0 + nt) % (times // 2) == 0:
                finish_half(t0 // (times // 2))

    for i in range(1, times):
        wait_part(summed, qsem, i)
    summed[tm] = acc[block(tm), :]
    total = summed[0]
    for t in range(1, times):
        total = total + summed[t]
    out_ref[...] = total

    def shift(j):
        odd = lax.rem(j, 2)
        return odd * ((j + 1) // 2) + (1 - odd) * lax.rem(times - j // 2, times)

    for h in range(2):

        def lag_part(step, _):
            high, low, thi, tlo = [], [], [], []
            for side in range(2):
                i = shift(2 * step + side)
                if side:
                    wait_part(parts.at[h], vsem.at[h], i)
                else:

                    @pl.when(step > 0)
                    def _():
                        wait_part(parts.at[h], vsem.at[h], i)

                t = lax.rem(tm + times - i, times)
                for part, into in zip(split(parts[h, t]), (high, low)):
                    into.append(part)
                thi.append(tbuf[t, 0, h * LANES : (h + 1) * LANES])
                tlo.append(tbuf[t, 1, h * LANES : (h + 1) * LANES])
            high, low = jnp.concatenate(high, axis=1), jnp.concatenate(low, axis=1)
            value = jnp.dot(jnp.concatenate([high, low]), jnp.concatenate(thi), preferred_element_type=F32)
            value = value[:share] + value[share:] + jnp.dot(high, jnp.concatenate(tlo), preferred_element_type=F32)
            out_ref[...] += value
            return 0

        lax.fori_loop(0, times // 2, lag_part, 0)
    out_ref[...] *= scale
    wait_given(acc, psem)
    for h in range(2):
        wait_given(stack.at[h], usem.at[h])
    others = sendbuf.at[late, :, :, pl.ds(0, (times - 1) * LANES)]
    pltpu.make_async_copy(others, others, esem.at[0]).wait()
    for c in range(len(chunks)):
        wait_sent(c)


def shards(first, added, spectra, send_rows, pair_list, pair_count):
    owners = lax.axis_size("pair")
    times = lax.axis_size("tm")
    channels, windows, _, bins = spectra.shape
    capacity = send_rows.shape[2]
    npairs = pair_list.shape[1]
    tiles = bins // LANES
    groups = tiles // GROUP
    lines = spectra.reshape(channels, windows, 2, tiles, LANES).transpose(0, 1, 3, 2, 4)
    lines = lines.reshape(channels, windows * tiles * 2, LANES)
    last = groups - 1
    chunks = [(g, 0, GROUP) for g in range(last - 1)]
    chunks += [(last - 1, 0, 4), (last - 1, 4, 2), (last - 1, 6, 2)]
    chunks += [(last, 0, 4), (last, 4, 2), (last, 6, 1), (last, 7, 1)]
    scale = (2.0 * bins * windows * times) ** (-0.5)
    dims = (owners, times, capacity, windows, groups, npairs, tuple(chunks), scale)
    rows = jnp.transpose(send_rows, (0, 2, 1)).reshape(capacity, owners)
    nc = len(chunks)
    dma = pltpu.SemaphoreType.DMA
    return pl.pallas_call(
        functools.partial(kernel, dims),
        out_shape=pltpu.VMEM((npairs // times, LAGS), F32),
        in_specs=[pl.BlockSpec(memory_space=pltpu.HBM)] * 6,
        out_specs=pl.BlockSpec(memory_space=pltpu.VMEM),
        scratch_shapes=[
            *[pltpu.VMEM((channels, windows * 2 * GROUP, LANES), BF16)] * groups,
            pltpu.SMEM(rows.shape, jnp.int32),
            pltpu.VMEM(pair_list.shape, jnp.int32),
            pltpu.SMEM((1,), jnp.int32),
            pltpu.VMEM((4 * 16 * GROUP, LANES), F32),
            pltpu.VMEM((groups, owners, 16, GROUP * LANES), BF16),
            pltpu.VMEM((owners, 16, GROUP * LANES), BF16),
            pltpu.VMEM((groups, owners, 16, GROUP * LANES), BF16),
            pltpu.VMEM((2, windows, npairs, 8 * owners), BF16),
            pltpu.VMEM((npairs, GROUP * 2 * LANES), BF16),
            pltpu.VMEM((npairs, GROUP * 2 * LANES), BF16),
            pltpu.VMEM((GROUP, 2, 2 * LANES, LAGS), BF16),
            pltpu.VMEM(first.shape, F32),
            pltpu.VMEM(added.shape, F32),
            pltpu.VMEM((npairs, LAGS), F32),
            pltpu.VMEM((times, npairs // times, LAGS), F32),
            pltpu.VMEM((2, npairs, LANES), F32),
            pltpu.VMEM((2, npairs, LANES), F32),
            pltpu.VMEM((2, times, npairs // times, LANES), F32),
            pltpu.VMEM((times, 16, LANES), BF16),
            dma((groups, windows)),
            dma((5,)),
            dma((nc,)),
            dma((nc,)),
            dma((nc,)),
            dma((3,)),
            dma,
            dma((times,)),
            dma((2,)),
            dma((2, times)),
        ],
        compiler_params=pltpu.CompilerParams(
            collective_id=0, has_side_effects=True, vmem_limit_bytes=58 * 1024 * 1024
        ),
        name="correlate",
    )(lines, rows, pair_list, pair_count, first, added)


def solution(mesh):
    first, added = lag_tables(4096, LAGS)

    def run(spectra, send_rows, pair_list, pair_count):
        in_specs = (P(), P(), P("pair", "tm", None, None), P("pair", None, None), P(None, "pair"), P("pair"))
        body = jax.shard_map(
            shards, mesh=mesh, in_specs=in_specs, out_specs=P(("pair", "tm"), None), check_vma=False
        )
        return body(jnp.asarray(first), jnp.asarray(added), spectra, send_rows, pair_list, pair_count)

    return run
```

```python
import functools
import math

import jax
import jax.numpy as jnp
import numpy as np
from jax import lax
from jax.experimental import pallas as pl
from jax.experimental.pallas import tpu as pltpu
from jax.sharding import PartitionSpec as P

MESH = pl.DeviceIdType.MESH
LAGS = 1024
LANES = 128
HALF = LANES // 2
GROUP = 8
F32 = jnp.float32
BF16 = jnp.bfloat16


def lag_tables(bins, lags):
    delay = np.arange(lags, dtype=np.int64) - lags // 2

    def pair(freq):
        angle = (freq[:, None] * delay[None, :] % (2 * bins)).astype(np.float64) * (math.pi / bins)
        return np.cos(angle).astype(np.float32), np.sin(angle).astype(np.float32)

    first = np.stack(pair(np.arange(bins // LANES, dtype=np.int64) * LANES), axis=1)
    added = np.stack(pair(np.arange(LANES, dtype=np.int64)))
    return first, added


def kernel(dims, x_hbm, rows_hbm, pairs_hbm, count_hbm, first_hbm, added_hbm, out_ref,
           *scratch):
    owners, times, capacity, windows, groups, npairs, chunks, scale = dims
    xbufs, scratch = scratch[:groups], scratch[groups:]
    rows_ref, pairs_ref, count_ref, stage, sendbuf, latebuf, recvbuf, ohot, scratch = *scratch[:8], scratch[8:]
    dhi, dlo, tbuf, first, added, acc, summed, sums, stack, parts, packed, scratch = *scratch[:11], scratch[11:]
    xsem, tsem, ssem, rsem, lsem, esem, psem, qsem, usem, vsem, rowsem = scratch
    late = groups - 1
    me = lax.axis_index("pair")
    tm = lax.axis_index("tm")
    share = npairs // times

    def load_x(g, w):
        rows = pl.ds((w * groups + g) * 2 * GROUP, 2 * GROUP)
        to = pl.ds(w * 2 * GROUP, 2 * GROUP)
        return pltpu.make_async_copy(x_hbm.at[:, rows, :], xbufs[g].at[:, to, :], xsem.at[g, w])

    def load_tables():
        return [
            pltpu.make_async_copy(pairs_hbm, pairs_ref, tsem.at[0]),
            pltpu.make_async_copy(count_hbm, count_ref, tsem.at[1]),
            pltpu.make_async_copy(first_hbm, first, tsem.at[2]),
            pltpu.make_async_copy(added_hbm, added, tsem.at[3]),
        ]

    rows_copy = pltpu.make_async_copy(rows_hbm, rows_ref, tsem.at[4])
    rows_copy.start()
    for w in range(windows):
        load_x(0, w).start()

    barrier = pltpu.get_barrier_semaphore()

    deep = 8
    wide = owners // deep
    y, z = me // deep, lax.rem(me, deep)

    def owner_at(dy, dz):
        return lax.rem(y + dy, wide) * deep + lax.rem(z + dz, deep)

    def near(i):
        along_y = i // deep
        return owner_at(along_y * lax.rem(i + 1, deep), (1 - along_y) * lax.rem(i, deep))

    def far(i):
        return owner_at(1 + i // (deep - 1), 1 + lax.rem(i, deep - 1))

    def greet_owner(i, _):
        pl.semaphore_signal(barrier, inc=1, device_id=(near(i), tm), device_id_type=MESH)
        return 0

    def greet_time(i, _):
        pl.semaphore_signal(barrier, inc=1, device_id=(me, lax.rem(tm + i, times)), device_id_type=MESH)
        return 0

    lax.fori_loop(1, deep + wide - 1, greet_owner, 0)
    lax.fori_loop(1, times, greet_time, 0)
    for g in range(1, groups):
        for w in range(windows):
            load_x(g, w).start()
    for copy in load_tables():
        copy.start()

    rows_copy.wait()

    def prepare(g):
        for w in range(windows):
            load_x(g, w).wait()

        def one(o, _):
            base = lax.rem(o, 4) * (16 * GROUP)
            for k in range(capacity):
                r = rows_ref[k, o]
                for w in range(windows):
                    v = xbufs[g][r, w * 2 * GROUP : (w + 1) * 2 * GROUP, :]
                    stage[pl.ds(base + k * windows + w, 2 * GROUP, stride=8), :] = v.astype(F32)
            for t in range(GROUP):
                sendbuf[g, o, :, t * LANES : (t + 1) * LANES] = stage[pl.ds(base + t * 16, 16), :].astype(BF16)
            return 0

        lax.fori_loop(0, owners, one, 0, unroll=2)

    def lanes(c):
        g, t0, nt = chunks[c]
        return pl.ds(t0 * LANES, nt * LANES)

    def source(g):
        return latebuf if g == late else sendbuf.at[g]

    def send(c):
        g = chunks[c][0]

        def start(to):
            pltpu.make_async_remote_copy(
                src_ref=source(g).at[to, :, lanes(c)], dst_ref=recvbuf.at[g, me, :, lanes(c)],
                send_sem=ssem.at[c], recv_sem=rsem.at[c], device_id=(to, tm), device_id_type=MESH,
            ).start()

        def one_near(i, _):
            start(near(i))
            return 0

        def one_far(i, _):
            start(far(i))
            return 0

        def pass_on(i, _):
            pl.semaphore_signal(rowsem, inc=1, device_id=(owner_at(i, 0), tm), device_id_type=MESH)
            return 0

        if c == 0:
            lax.fori_loop(1, wide, pass_on, 0)
        lax.fori_loop(1, deep + wide - 1, one_near, 0)
        if c == 0:
            pl.semaphore_wait(rowsem, wide - 1)
        lax.fori_loop(0, (deep - 1) * (wide - 1), one_far, 0)
        pltpu.make_async_copy(source(g).at[me, :, lanes(c)], recvbuf.at[g, me, :, lanes(c)], lsem.at[c]).start()

    def wait_received(c):
        g = chunks[c][0]
        others = recvbuf.at[g, pl.ds(0, owners - 1), :, lanes(c)]
        pltpu.make_async_copy(others, others, rsem.at[c]).wait()
        own = recvbuf.at[g, me, :, lanes(c)]
        pltpu.make_async_copy(own, own, lsem.at[c]).wait()

    def wait_sent(c):
        g = chunks[c][0]
        others = source(g).at[pl.ds(0, owners - 1), :, lanes(c)]
        pltpu.make_async_copy(others, others, ssem.at[c]).wait()

    def tile(t):
        return pl.ds(pl.multiple_of(t * LANES, LANES), LANES)

    own_tile = pltpu.make_async_copy(sendbuf.at[late, :, :, tile(tm)], latebuf.at[:, :, tile(tm)], esem.at[2])

    def trade():
        def one(i, _):
            to = lax.rem(tm + i, times)
            pltpu.make_async_remote_copy(
                src_ref=sendbuf.at[late, :, :, tile(to)], dst_ref=latebuf.at[:, :, tile(tm)],
                send_sem=esem.at[0], recv_sem=esem.at[1], device_id=(me, to), device_id_type=MESH,
            ).start()
            return 0

        lax.fori_loop(1, times, one, 0)
        own_tile.start()

    def wait_traded():
        others = latebuf.at[:, :, pl.ds(0, (times - 1) * LANES)]
        pltpu.make_async_copy(others, others, esem.at[1]).wait()
        own_tile.wait()

        def pack(o, _):
            for row in range(times // 2):
                x = latebuf[o, :, row * 2 * LANES : (row * 2 + 1) * LANES].astype(F32)
                y = latebuf[o, :, (row * 2 + 1) * LANES : (row * 2 + 2) * LANES].astype(F32)
                for h in range(2):
                    cut = slice(h * HALF, (h + 1) * HALF)
                    packed[h * (times // 2) + row] = jnp.concatenate([x[:, cut], y[:, cut]], axis=1).astype(BF16)
            for t in range(times):
                latebuf[o, :, t * LANES : (t + 1) * LANES] = packed[t]
            return 0

        lax.fori_loop(0, owners, pack, 0)

    for g in (0, late, *range(1, late)):
        prepare(g)
        if g == 0:
            pl.semaphore_wait(barrier, deep + wide - 2 + times - 1)
        if g == late:
            trade()
        for c in range(len(chunks)):
            if chunks[c][0] == g < late:
                send(c)

    for copy in load_tables():
        copy.wait()

    lines = 8 * owners
    column = lax.broadcasted_iota(jnp.int32, (npairs, lines), 1)
    slot = lax.broadcasted_iota(jnp.int32, (npairs, lines), 0)
    live = slot < count_ref[0]
    for side in range(2):
        ids = jnp.transpose(jnp.broadcast_to(pairs_ref[side : side + 1, :], (LANES, npairs)))
        line = jnp.concatenate([ids * windows] * (lines // LANES), axis=1)
        for w in range(windows):
            hit = column == line + w
            if side == 0:
                hit = hit & live
            ohot[side, w] = jnp.where(hit, 1.0, 0.0).astype(F32).astype(BF16)

    acc[...] = jnp.zeros(acc.shape, F32)

    def split(value):
        high = value.astype(BF16)
        return high, (value - high.astype(F32)).astype(BF16)

    def make_table(g):
        def one(i, _):
            t, n = i // (LAGS // 256), lax.rem(i, LAGS // 256)
            at = pl.ds(pl.multiple_of(n * 256, 256), 256)
            c0, s0 = first[g * GROUP + t, 0:1, at], first[g * GROUP + t, 1:2, at]
            c1, s1 = added[0, :, at], added[1, :, at]
            for part, value in enumerate((c0 * c1 - s0 * s1, -(s0 * c1 + c0 * s1))):
                for i, piece in enumerate(split(value)):
                    if g == late:
                        for h in range(2):
                            row = h * LANES + part * HALF
                            tbuf[t, i, row : row + HALF, at] = piece[h * HALF : (h + 1) * HALF]
                    else:
                        tbuf[t, i, part * LANES : (part + 1) * LANES, at] = piece
            return 0

        lax.fori_loop(0, GROUP * (LAGS // 256), one, 0)

    def cross(g, at, width):
        both = recvbuf[g, :, :, pl.ds(at, width)].astype(F32)
        rows = [both[:, part * 8 : part * 8 + 8, :].reshape(8 * owners, width).astype(BF16) for part in range(2)]
        rows = jnp.concatenate(rows, axis=1)
        real = None
        for w in range(windows):
            a = jnp.dot(ohot[0, w], rows, preferred_element_type=F32)
            b = jnp.dot(ohot[1, w], rows, preferred_element_type=F32)
            a, b = [(v[:, :width], v[:, width:]) for v in (a, b)]
            re = a[0] * b[0] + a[1] * b[1]
            im = a[1] * b[0] - a[0] * b[1]
            real, imag = (re, im) if real is None else (real + re, imag + im)
        return real, imag

    def early_chunk(g, t0, nt):
        def piece(i, _):
            at = pl.multiple_of((t0 + 2 * i) * LANES, 2 * LANES)
            for part, value in enumerate(cross(g, at, 2 * LANES)):
                high, low = split(value)
                for t in range(2):
                    to = pl.ds(pl.multiple_of((2 * i + t) * 2 * LANES, 2 * LANES) + part * LANES, LANES)
                    dhi[:, to] = high[:, t * LANES : (t + 1) * LANES]
                    dlo[:, to] = low[:, t * LANES : (t + 1) * LANES]
            return 0

        lax.fori_loop(0, nt // 2, piece, 0)
        depth = nt * 2 * LANES

        def lag_tile(n, _):
            at = pl.ds(pl.multiple_of(n * 256, 256), 256)
            thi = tbuf[t0 : t0 + nt, 0, :, at].reshape(depth, 256)
            tlo = tbuf[t0 : t0 + nt, 1, :, at].reshape(depth, 256)
            high = dhi[:, :depth]
            total = jnp.dot(high, thi, preferred_element_type=F32)
            total += jnp.dot(dlo[:, :depth], thi, preferred_element_type=F32)
            total += jnp.dot(high, tlo, preferred_element_type=F32)
            acc[:, at] += total
            return 0

        lax.fori_loop(0, LAGS // 256, lag_tile, 0)

    def late_chunk(t0, nt):
        def piece(i, _):
            at = pl.multiple_of((t0 + 2 * i) * LANES, 2 * LANES)
            for part, value in enumerate(cross(late, at, 2 * LANES)):
                sums[part] += value[:, :LANES] + value[:, LANES:]
            return 0

        if t0 % (times // 2) == 0:
            sums[...] = jnp.zeros(sums.shape, F32)
        if nt > 1:
            lax.fori_loop(0, nt // 2, piece, 0)
        else:
            for part, value in enumerate(cross(late, t0 * LANES, LANES)):
                sums[part] += value

    def finish_half(h):
        halves = [sums[part, :, :HALF] + sums[part, :, HALF:] for part in range(2)]
        stack[h] = jnp.concatenate(halves, axis=1)
        give(stack.at[h], parts.at[h], usem.at[h], vsem.at[h])
        parts[h, tm] = stack[h, block(tm), :]

    def block(t):
        return pl.ds(pl.multiple_of(t * share, 8), share)

    def give(src, dst, send_sem, recv_sem):
        def one(i, _):
            far = lax.rem(i, 2) * (times // 2 + (i - 1) // 2) + (1 - lax.rem(i, 2)) * (times // 2 - i // 2)
            to = lax.rem(tm + far, times)
            pltpu.make_async_remote_copy(
                src_ref=src.at[block(to), :], dst_ref=dst.at[tm], send_sem=send_sem, recv_sem=recv_sem.at[far],
                device_id=(me, to), device_id_type=MESH,
            ).start()
            return 0

        lax.fori_loop(1, times, one, 0)

    def wait_given(src, sem):
        given = src.at[pl.ds(0, (times - 1) * share), :]
        pltpu.make_async_copy(given, given, sem).wait()

    def wait_part(dst, sem, i):
        come = dst.at[lax.rem(tm + times - i, times)]
        pltpu.make_async_copy(come, come, sem.at[i]).wait()

    for c, (g, t0, nt) in enumerate(chunks):
        if t0 == 0:
            make_table(g)
        if c == 1:
            wait_traded()
            for d in range(len(chunks)):
                if chunks[d][0] == late:
                    send(d)
        wait_received(c)
        if g < late:
            early_chunk(g, t0, nt)
            if chunks[c + 1][0] == late:
                give(acc, summed, psem, qsem)
        else:
            late_chunk(t0, nt)
            if (t0 + nt) % (times // 2) == 0:
                finish_half(t0 // (times // 2))

    for i in range(1, times):
        wait_part(summed, qsem, i)
    summed[tm] = acc[block(tm), :]
    total = summed[0]
    for t in range(1, times):
        total = total + summed[t]
    out_ref[...] = total

    def shift(j):
        odd = lax.rem(j, 2)
        return odd * ((j + 1) // 2) + (1 - odd) * lax.rem(times - j // 2, times)

    for h in range(2):

        def lag_part(step, _):
            high, low, thi, tlo = [], [], [], []
            for side in range(2):
                i = shift(2 * step + side)
                if side:
                    wait_part(parts.at[h], vsem.at[h], i)
                else:

                    @pl.when(step > 0)
                    def _():
                        wait_part(parts.at[h], vsem.at[h], i)

                t = lax.rem(tm + times - i, times)
                for part, into in zip(split(parts[h, t]), (high, low)):
                    into.append(part)
                thi.append(tbuf[t, 0, h * LANES : (h + 1) * LANES])
                tlo.append(tbuf[t, 1, h * LANES : (h + 1) * LANES])
            high, low = jnp.concatenate(high, axis=1), jnp.concatenate(low, axis=1)
            value = jnp.dot(jnp.concatenate([high, low]), jnp.concatenate(thi), preferred_element_type=F32)
            value = value[:share] + value[share:] + jnp.dot(high, jnp.concatenate(tlo), preferred_element_type=F32)
            out_ref[...] += value
            return 0

        lax.fori_loop(0, times // 2, lag_part, 0)
    out_ref[...] *= scale
    wait_given(acc, psem)
    for h in range(2):
        wait_given(stack.at[h], usem.at[h])
    others = sendbuf.at[late, :, :, pl.ds(0, (times - 1) * LANES)]
    pltpu.make_async_copy(others, others, esem.at[0]).wait()
    for c in range(len(chunks)):
        wait_sent(c)


def shards(first, added, spectra, send_rows, pair_list, pair_count):
    owners = lax.axis_size("pair")
    times = lax.axis_size("tm")
    channels, windows, _, bins = spectra.shape
    capacity = send_rows.shape[2]
    npairs = pair_list.shape[1]
    tiles = bins // LANES
    groups = tiles // GROUP
    lines = spectra.reshape(channels, windows, 2, tiles, LANES).transpose(0, 1, 3, 2, 4)
    lines = lines.reshape(channels, windows * tiles * 2, LANES)
    last = groups - 1
    chunks = [(g, 0, GROUP) for g in range(last - 1)]
    chunks += [(last - 1, a, b) for a, b in [(0, 4), (4, 4)]]
    chunks += [(last, a, b) for a, b in [(0, 4), (4, 2), (6, 2)]]
    scale = (2.0 * bins * windows * times) ** (-0.5)
    dims = (owners, times, capacity, windows, groups, npairs, tuple(chunks), scale)
    rows = jnp.transpose(send_rows, (0, 2, 1)).reshape(capacity, owners)
    nc = len(chunks)
    dma = pltpu.SemaphoreType.DMA
    return pl.pallas_call(
        functools.partial(kernel, dims),
        out_shape=pltpu.VMEM((npairs // times, LAGS), F32),
        in_specs=[pl.BlockSpec(memory_space=pltpu.HBM)] * 6,
        out_specs=pl.BlockSpec(memory_space=pltpu.VMEM),
        scratch_shapes=[
            *[pltpu.VMEM((channels, windows * 2 * GROUP, LANES), BF16)] * groups,
            pltpu.SMEM(rows.shape, jnp.int32),
            pltpu.VMEM(pair_list.shape, jnp.int32),
            pltpu.SMEM((1,), jnp.int32),
            pltpu.VMEM((4 * 16 * GROUP, LANES), F32),
            pltpu.VMEM((groups, owners, 16, GROUP * LANES), BF16),
            pltpu.VMEM((owners, 16, GROUP * LANES), BF16),
            pltpu.VMEM((groups, owners, 16, GROUP * LANES), BF16),
            pltpu.VMEM((2, windows, npairs, 8 * owners), BF16),
            pltpu.VMEM((npairs, GROUP * 2 * LANES), BF16),
            pltpu.VMEM((npairs, GROUP * 2 * LANES), BF16),
            pltpu.VMEM((GROUP, 2, 2 * LANES, LAGS), BF16),
            pltpu.VMEM(first.shape, F32),
            pltpu.VMEM(added.shape, F32),
            pltpu.VMEM((npairs, LAGS), F32),
            pltpu.VMEM((times, npairs // times, LAGS), F32),
            pltpu.VMEM((2, npairs, LANES), F32),
            pltpu.VMEM((2, npairs, LANES), F32),
            pltpu.VMEM((2, times, npairs // times, LANES), F32),
            pltpu.VMEM((times, 16, LANES), BF16),
            dma((groups, windows)),
            dma((5,)),
            dma((nc,)),
            dma((nc,)),
            dma((nc,)),
            dma((3,)),
            dma,
            dma((times,)),
            dma((2,)),
            dma((2, times)),
            pltpu.SemaphoreType.REGULAR,
        ],
        compiler_params=pltpu.CompilerParams(
            collective_id=0, has_side_effects=True, vmem_limit_bytes=58 * 1024 * 1024
        ),
        name="correlate",
    )(lines, rows, pair_list, pair_count, first, added)


def solution(mesh):
    first, added = lag_tables(4096, LAGS)

    def run(spectra, send_rows, pair_list, pair_count):
        in_specs = (P(), P(), P("pair", "tm", None, None), P("pair", None, None), P(None, "pair"), P("pair"))
        body = jax.shard_map(
            shards, mesh=mesh, in_specs=in_specs, out_specs=P(("pair", "tm"), None), check_vma=False
        )
        return body(jnp.asarray(first), jnp.asarray(added), spectra, send_rows, pair_list, pair_count)

    return run
```

```python
import functools
import math

import jax
import jax.numpy as jnp
import numpy as np
from jax import lax
from jax.experimental import pallas as pl
from jax.experimental.pallas import tpu as pltpu
from jax.sharding import PartitionSpec as P

MESH = pl.DeviceIdType.MESH
LAGS = 1024
LANES = 128
HALF = LANES // 2
GROUP = 8
F32 = jnp.float32
BF16 = jnp.bfloat16


def lag_tables(bins, lags):
    delay = np.arange(lags, dtype=np.int64) - lags // 2

    def pair(freq):
        angle = (freq[:, None] * delay[None, :] % (2 * bins)).astype(np.float64) * (math.pi / bins)
        return np.cos(angle).astype(np.float32), np.sin(angle).astype(np.float32)

    first = np.stack(pair(np.arange(bins // LANES, dtype=np.int64) * LANES), axis=1)
    added = np.stack(pair(np.arange(LANES, dtype=np.int64)))
    return first, added


def kernel(dims, x_hbm, rows_hbm, pairs_hbm, count_hbm, first_hbm, added_hbm, out_ref,
           *scratch):
    owners, times, capacity, windows, groups, npairs, chunks, scale = dims
    xbufs, scratch = scratch[:groups], scratch[groups:]
    rows_ref, pairs_ref, count_ref, stage, sendbuf, latebuf, recvbuf, ohot, scratch = *scratch[:8], scratch[8:]
    dhi, dlo, tbuf, first, added, acc, summed, sums, stack, parts, packed, scratch = *scratch[:11], scratch[11:]
    xsem, tsem, ssem, rsem, lsem, esem, psem, qsem, usem, vsem, rowsem = scratch
    late = groups - 1
    me = lax.axis_index("pair")
    tm = lax.axis_index("tm")
    share = npairs // times

    def load_x(g, w):
        rows = pl.ds((w * groups + g) * 2 * GROUP, 2 * GROUP)
        to = pl.ds(w * 2 * GROUP, 2 * GROUP)
        return pltpu.make_async_copy(x_hbm.at[:, rows, :], xbufs[g].at[:, to, :], xsem.at[g, w])

    def load_tables():
        return [
            pltpu.make_async_copy(pairs_hbm, pairs_ref, tsem.at[0]),
            pltpu.make_async_copy(count_hbm, count_ref, tsem.at[1]),
            pltpu.make_async_copy(first_hbm, first, tsem.at[2]),
            pltpu.make_async_copy(added_hbm, added, tsem.at[3]),
        ]

    rows_copy = pltpu.make_async_copy(rows_hbm, rows_ref, tsem.at[4])
    rows_copy.start()
    for w in range(windows):
        load_x(0, w).start()

    barrier = pltpu.get_barrier_semaphore()

    deep = 8
    wide = owners // deep
    y, z = me // deep, lax.rem(me, deep)

    def owner_at(dy, dz):
        return lax.rem(y + dy, wide) * deep + lax.rem(z + dz, deep)

    def near(i):
        along_y = i // deep
        return owner_at(along_y * lax.rem(i + 1, deep), (1 - along_y) * lax.rem(i, deep))

    def far(i):
        return owner_at(1 + i // (deep - 1), 1 + lax.rem(i, deep - 1))

    def greet_owner(i, _):
        pl.semaphore_signal(barrier, inc=1, device_id=(near(i), tm), device_id_type=MESH)
        return 0

    def greet_time(i, _):
        pl.semaphore_signal(barrier, inc=1, device_id=(me, lax.rem(tm + i, times)), device_id_type=MESH)
        return 0

    lax.fori_loop(1, deep + wide - 1, greet_owner, 0)
    lax.fori_loop(1, times, greet_time, 0)
    for g in range(1, groups):
        for w in range(windows):
            load_x(g, w).start()
    for copy in load_tables():
        copy.start()

    rows_copy.wait()

    def prepare(g):
        for w in range(windows):
            load_x(g, w).wait()

        def one(o, _):
            base = lax.rem(o, 4) * (16 * GROUP)
            for k in range(capacity):
                r = rows_ref[k, o]
                for w in range(windows):
                    v = xbufs[g][r, w * 2 * GROUP : (w + 1) * 2 * GROUP, :]
                    stage[pl.ds(base + k * windows + w, 2 * GROUP, stride=8), :] = v.astype(F32)
            for t in range(GROUP):
                sendbuf[g, o, :, t * LANES : (t + 1) * LANES] = stage[pl.ds(base + t * 16, 16), :].astype(BF16)
            return 0

        lax.fori_loop(0, owners, one, 0, unroll=2)

    def lanes(c):
        g, t0, nt = chunks[c]
        return pl.ds(t0 * LANES, nt * LANES)

    def source(g):
        return latebuf if g == late else sendbuf.at[g]

    def send(c):
        g = chunks[c][0]

        def start(to):
            pltpu.make_async_remote_copy(
                src_ref=source(g).at[to, :, lanes(c)], dst_ref=recvbuf.at[g, me, :, lanes(c)],
                send_sem=ssem.at[c], recv_sem=rsem.at[c], device_id=(to, tm), device_id_type=MESH,
            ).start()

        def one_near(i, _):
            start(near(i))
            return 0

        def one_far(i, _):
            start(far(i))
            return 0

        def pass_on(i, _):
            pl.semaphore_signal(rowsem, inc=1, device_id=(owner_at(i, 0), tm), device_id_type=MESH)
            return 0

        if c == 0:
            lax.fori_loop(1, wide, pass_on, 0)
            lax.fori_loop(1, deep + wide - 1, one_near, 0)
            pl.semaphore_wait(rowsem, wide - 1)
        lax.fori_loop(0, (deep - 1) * (wide - 1), one_far, 0)
        if c:
            lax.fori_loop(1, deep + wide - 1, one_near, 0)
        pltpu.make_async_copy(source(g).at[me, :, lanes(c)], recvbuf.at[g, me, :, lanes(c)], lsem.at[c]).start()

    def wait_received(c):
        g = chunks[c][0]
        others = recvbuf.at[g, pl.ds(0, owners - 1), :, lanes(c)]
        pltpu.make_async_copy(others, others, rsem.at[c]).wait()
        own = recvbuf.at[g, me, :, lanes(c)]
        pltpu.make_async_copy(own, own, lsem.at[c]).wait()

    def wait_sent(c):
        g = chunks[c][0]
        others = source(g).at[pl.ds(0, owners - 1), :, lanes(c)]
        pltpu.make_async_copy(others, others, ssem.at[c]).wait()

    def tile(t):
        return pl.ds(pl.multiple_of(t * LANES, LANES), LANES)

    own_tile = pltpu.make_async_copy(sendbuf.at[late, :, :, tile(tm)], latebuf.at[:, :, tile(tm)], esem.at[2])

    def trade():
        def one(i, _):
            to = lax.rem(tm + i, times)
            pltpu.make_async_remote_copy(
                src_ref=sendbuf.at[late, :, :, tile(to)], dst_ref=latebuf.at[:, :, tile(tm)],
                send_sem=esem.at[0], recv_sem=esem.at[1], device_id=(me, to), device_id_type=MESH,
            ).start()
            return 0

        lax.fori_loop(1, times, one, 0)
        own_tile.start()

    def wait_traded():
        others = latebuf.at[:, :, pl.ds(0, (times - 1) * LANES)]
        pltpu.make_async_copy(others, others, esem.at[1]).wait()
        own_tile.wait()

        def pack(o, _):
            for row in range(times // 2):
                x = latebuf[o, :, row * 2 * LANES : (row * 2 + 1) * LANES].astype(F32)
                y = latebuf[o, :, (row * 2 + 1) * LANES : (row * 2 + 2) * LANES].astype(F32)
                for h in range(2):
                    cut = slice(h * HALF, (h + 1) * HALF)
                    packed[h * (times // 2) + row] = jnp.concatenate([x[:, cut], y[:, cut]], axis=1).astype(BF16)
            for t in range(times):
                latebuf[o, :, t * LANES : (t + 1) * LANES] = packed[t]
            return 0

        lax.fori_loop(0, owners, pack, 0)

    for g in (0, late, *range(1, late)):
        prepare(g)
        if g == 0:
            pl.semaphore_wait(barrier, deep + wide - 2 + times - 1)
        if g == late:
            trade()
        for c in range(len(chunks)):
            if chunks[c][0] == g < late:
                send(c)

    for copy in load_tables():
        copy.wait()

    lines = 8 * owners
    column = lax.broadcasted_iota(jnp.int32, (npairs, lines), 1)
    slot = lax.broadcasted_iota(jnp.int32, (npairs, lines), 0)
    live = slot < count_ref[0]
    for side in range(2):
        ids = jnp.transpose(jnp.broadcast_to(pairs_ref[side : side + 1, :], (LANES, npairs)))
        line = jnp.concatenate([ids * windows] * (lines // LANES), axis=1)
        for w in range(windows):
            hit = column == line + w
            if side == 0:
                hit = hit & live
            ohot[side, w] = jnp.where(hit, 1.0, 0.0).astype(F32).astype(BF16)

    acc[...] = jnp.zeros(acc.shape, F32)

    def split(value):
        high = value.astype(BF16)
        return high, (value - high.astype(F32)).astype(BF16)

    def make_table(g):
        def one(i, _):
            t, n = i // (LAGS // 256), lax.rem(i, LAGS // 256)
            at = pl.ds(pl.multiple_of(n * 256, 256), 256)
            c0, s0 = first[g * GROUP + t, 0:1, at], first[g * GROUP + t, 1:2, at]
            c1, s1 = added[0, :, at], added[1, :, at]
            for part, value in enumerate((c0 * c1 - s0 * s1, -(s0 * c1 + c0 * s1))):
                for i, piece in enumerate(split(value)):
                    if g == late:
                        for h in range(2):
                            row = h * LANES + part * HALF
                            tbuf[t, i, row : row + HALF, at] = piece[h * HALF : (h + 1) * HALF]
                    else:
                        tbuf[t, i, part * LANES : (part + 1) * LANES, at] = piece
            return 0

        lax.fori_loop(0, GROUP * (LAGS // 256), one, 0)

    def cross(g, at, width):
        both = recvbuf[g, :, :, pl.ds(at, width)].astype(F32)
        rows = [both[:, part * 8 : part * 8 + 8, :].reshape(8 * owners, width).astype(BF16) for part in range(2)]
        rows = jnp.concatenate(rows, axis=1)
        real = None
        for w in range(windows):
            a = jnp.dot(ohot[0, w], rows, preferred_element_type=F32)
            b = jnp.dot(ohot[1, w], rows, preferred_element_type=F32)
            a, b = [(v[:, :width], v[:, width:]) for v in (a, b)]
            re = a[0] * b[0] + a[1] * b[1]
            im = a[1] * b[0] - a[0] * b[1]
            real, imag = (re, im) if real is None else (real + re, imag + im)
        return real, imag

    def early_chunk(g, t0, nt):
        def piece(i, _):
            at = pl.multiple_of((t0 + 2 * i) * LANES, 2 * LANES)
            for part, value in enumerate(cross(g, at, 2 * LANES)):
                high, low = split(value)
                for t in range(2):
                    to = pl.ds(pl.multiple_of((2 * i + t) * 2 * LANES, 2 * LANES) + part * LANES, LANES)
                    dhi[:, to] = high[:, t * LANES : (t + 1) * LANES]
                    dlo[:, to] = low[:, t * LANES : (t + 1) * LANES]
            return 0

        lax.fori_loop(0, nt // 2, piece, 0)
        depth = nt * 2 * LANES

        def lag_tile(n, _):
            at = pl.ds(pl.multiple_of(n * 256, 256), 256)
            thi = tbuf[t0 : t0 + nt, 0, :, at].reshape(depth, 256)
            tlo = tbuf[t0 : t0 + nt, 1, :, at].reshape(depth, 256)
            high = dhi[:, :depth]
            total = jnp.dot(high, thi, preferred_element_type=F32)
            total += jnp.dot(dlo[:, :depth], thi, preferred_element_type=F32)
            total += jnp.dot(high, tlo, preferred_element_type=F32)
            acc[:, at] += total
            return 0

        lax.fori_loop(0, LAGS // 256, lag_tile, 0)

    def late_chunk(t0, nt):
        def piece(i, _):
            at = pl.multiple_of((t0 + 2 * i) * LANES, 2 * LANES)
            for part, value in enumerate(cross(late, at, 2 * LANES)):
                sums[part] += value[:, :LANES] + value[:, LANES:]
            return 0

        if t0 % (times // 2) == 0:
            sums[...] = jnp.zeros(sums.shape, F32)
        if nt > 1:
            lax.fori_loop(0, nt // 2, piece, 0)
        else:
            for part, value in enumerate(cross(late, t0 * LANES, LANES)):
                sums[part] += value

    def finish_half(h):
        halves = [sums[part, :, :HALF] + sums[part, :, HALF:] for part in range(2)]
        stack[h] = jnp.concatenate(halves, axis=1)
        give(stack.at[h], parts.at[h], usem.at[h], vsem.at[h])
        parts[h, tm] = stack[h, block(tm), :]

    def block(t):
        return pl.ds(pl.multiple_of(t * share, 8), share)

    def give(src, dst, send_sem, recv_sem):
        def one(i, _):
            far = lax.rem(i, 2) * (times // 2 + (i - 1) // 2) + (1 - lax.rem(i, 2)) * (times // 2 - i // 2)
            to = lax.rem(tm + far, times)
            pltpu.make_async_remote_copy(
                src_ref=src.at[block(to), :], dst_ref=dst.at[tm], send_sem=send_sem, recv_sem=recv_sem.at[far],
                device_id=(me, to), device_id_type=MESH,
            ).start()
            return 0

        lax.fori_loop(1, times, one, 0)

    def wait_given(src, sem):
        given = src.at[pl.ds(0, (times - 1) * share), :]
        pltpu.make_async_copy(given, given, sem).wait()

    def wait_part(dst, sem, i):
        come = dst.at[lax.rem(tm + times - i, times)]
        pltpu.make_async_copy(come, come, sem.at[i]).wait()

    for c, (g, t0, nt) in enumerate(chunks):
        if t0 == 0:
            make_table(g)
        if c == 1:
            wait_traded()
            for d in range(len(chunks)):
                if chunks[d][0] == late:
                    send(d)
        wait_received(c)
        if g < late:
            early_chunk(g, t0, nt)
            if chunks[c + 1][0] == late:
                give(acc, summed, psem, qsem)
        else:
            late_chunk(t0, nt)
            if (t0 + nt) % (times // 2) == 0:
                finish_half(t0 // (times // 2))

    for i in range(1, times):
        wait_part(summed, qsem, i)
    summed[tm] = acc[block(tm), :]
    total = summed[0]
    for t in range(1, times):
        total = total + summed[t]
    out_ref[...] = total

    def shift(j):
        odd = lax.rem(j, 2)
        return odd * ((j + 1) // 2) + (1 - odd) * lax.rem(times - j // 2, times)

    for h in range(2):

        def lag_part(step, _):
            high, low, thi, tlo = [], [], [], []
            for side in range(2):
                i = shift(2 * step + side)
                if side:
                    wait_part(parts.at[h], vsem.at[h], i)
                else:

                    @pl.when(step > 0)
                    def _():
                        wait_part(parts.at[h], vsem.at[h], i)

                t = lax.rem(tm + times - i, times)
                for part, into in zip(split(parts[h, t]), (high, low)):
                    into.append(part)
                thi.append(tbuf[t, 0, h * LANES : (h + 1) * LANES])
                tlo.append(tbuf[t, 1, h * LANES : (h + 1) * LANES])
            high, low = jnp.concatenate(high, axis=1), jnp.concatenate(low, axis=1)
            value = jnp.dot(jnp.concatenate([high, low]), jnp.concatenate(thi), preferred_element_type=F32)
            value = value[:share] + value[share:] + jnp.dot(high, jnp.concatenate(tlo), preferred_element_type=F32)
            out_ref[...] += value
            return 0

        lax.fori_loop(0, times // 2, lag_part, 0)
    out_ref[...] *= scale
    wait_given(acc, psem)
    for h in range(2):
        wait_given(stack.at[h], usem.at[h])
    others = sendbuf.at[late, :, :, pl.ds(0, (times - 1) * LANES)]
    pltpu.make_async_copy(others, others, esem.at[0]).wait()
    for c in range(len(chunks)):
        wait_sent(c)


def shards(first, added, spectra, send_rows, pair_list, pair_count):
    owners = lax.axis_size("pair")
    times = lax.axis_size("tm")
    channels, windows, _, bins = spectra.shape
    capacity = send_rows.shape[2]
    npairs = pair_list.shape[1]
    tiles = bins // LANES
    groups = tiles // GROUP
    lines = spectra.reshape(channels, windows, 2, tiles, LANES).transpose(0, 1, 3, 2, 4)
    lines = lines.reshape(channels, windows * tiles * 2, LANES)
    last = groups - 1
    chunks = [(g, 0, GROUP) for g in range(last - 1)]
    chunks += [(last - 1, a, b) for a, b in [(0, 4), (4, 4)]]
    chunks += [(last, a, b) for a, b in [(0, 4), (4, 2), (6, 2)]]
    scale = (2.0 * bins * windows * times) ** (-0.5)
    dims = (owners, times, capacity, windows, groups, npairs, tuple(chunks), scale)
    rows = jnp.transpose(send_rows, (0, 2, 1)).reshape(capacity, owners)
    nc = len(chunks)
    dma = pltpu.SemaphoreType.DMA
    return pl.pallas_call(
        functools.partial(kernel, dims),
        out_shape=pltpu.VMEM((npairs // times, LAGS), F32),
        in_specs=[pl.BlockSpec(memory_space=pltpu.HBM)] * 6,
        out_specs=pl.BlockSpec(memory_space=pltpu.VMEM),
        scratch_shapes=[
            *[pltpu.VMEM((channels, windows * 2 * GROUP, LANES), BF16)] * groups,
            pltpu.SMEM(rows.shape, jnp.int32),
            pltpu.VMEM(pair_list.shape, jnp.int32),
            pltpu.SMEM((1,), jnp.int32),
            pltpu.VMEM((4 * 16 * GROUP, LANES), F32),
            pltpu.VMEM((groups, owners, 16, GROUP * LANES), BF16),
            pltpu.VMEM((owners, 16, GROUP * LANES), BF16),
            pltpu.VMEM((groups, owners, 16, GROUP * LANES), BF16),
            pltpu.VMEM((2, windows, npairs, 8 * owners), BF16),
            pltpu.VMEM((npairs, GROUP * 2 * LANES), BF16),
            pltpu.VMEM((npairs, GROUP * 2 * LANES), BF16),
            pltpu.VMEM((GROUP, 2, 2 * LANES, LAGS), BF16),
            pltpu.VMEM(first.shape, F32),
            pltpu.VMEM(added.shape, F32),
            pltpu.VMEM((npairs, LAGS), F32),
            pltpu.VMEM((times, npairs // times, LAGS), F32),
            pltpu.VMEM((2, npairs, LANES), F32),
            pltpu.VMEM((2, npairs, LANES), F32),
            pltpu.VMEM((2, times, npairs // times, LANES), F32),
            pltpu.VMEM((times, 16, LANES), BF16),
            dma((groups, windows)),
            dma((5,)),
            dma((nc,)),
            dma((nc,)),
            dma((nc,)),
            dma((3,)),
            dma,
            dma((times,)),
            dma((2,)),
            dma((2, times)),
            pltpu.SemaphoreType.REGULAR,
        ],
        compiler_params=pltpu.CompilerParams(
            collective_id=0, has_side_effects=True, vmem_limit_bytes=58 * 1024 * 1024
        ),
        name="correlate",
    )(lines, rows, pair_list, pair_count, first, added)


def solution(mesh):
    first, added = lag_tables(4096, LAGS)

    def run(spectra, send_rows, pair_list, pair_count):
        in_specs = (P(), P(), P("pair", "tm", None, None), P("pair", None, None), P(None, "pair"), P("pair"))
        body = jax.shard_map(
            shards, mesh=mesh, in_specs=in_specs, out_specs=P(("pair", "tm"), None), check_vma=False
        )
        return body(jnp.asarray(first), jnp.asarray(added), spectra, send_rows, pair_list, pair_count)

    return run
```

```python
import functools
import math

import jax
import jax.numpy as jnp
import numpy as np
from jax import lax
from jax.experimental import pallas as pl
from jax.experimental.pallas import tpu as pltpu
from jax.sharding import PartitionSpec as P

MESH = pl.DeviceIdType.MESH
LAGS = 1024
LANES = 128
HALF = LANES // 2
GROUP = 8
F32 = jnp.float32
BF16 = jnp.bfloat16


def lag_tables(bins, lags):
    delay = np.arange(lags, dtype=np.int64) - lags // 2

    def pair(freq):
        angle = (freq[:, None] * delay[None, :] % (2 * bins)).astype(np.float64) * (math.pi / bins)
        return np.cos(angle).astype(np.float32), np.sin(angle).astype(np.float32)

    first = np.stack(pair(np.arange(bins // LANES, dtype=np.int64) * LANES), axis=1)
    added = np.stack(pair(np.arange(LANES, dtype=np.int64)))
    return first, added


def kernel(dims, x_hbm, rows_hbm, pairs_hbm, count_hbm, first_hbm, added_hbm, out_ref,
           *scratch):
    owners, times, capacity, windows, groups, npairs, chunks, scale = dims
    xbufs, scratch = scratch[:groups], scratch[groups:]
    rows_ref, pairs_ref, count_ref, stage, sendbuf, latebuf, recvbuf, ohot, scratch = *scratch[:8], scratch[8:]
    dhi, dlo, tbuf, first, added, acc, summed, sums, stack, parts, packed, scratch = *scratch[:11], scratch[11:]
    xsem, tsem, ssem, rsem, lsem, esem, psem, qsem, usem, vsem, rowsem = scratch
    late = groups - 1
    me = lax.axis_index("pair")
    tm = lax.axis_index("tm")
    share = npairs // times

    def load_x(g, w):
        rows = pl.ds((w * groups + g) * 2 * GROUP, 2 * GROUP)
        to = pl.ds(w * 2 * GROUP, 2 * GROUP)
        return pltpu.make_async_copy(x_hbm.at[:, rows, :], xbufs[g].at[:, to, :], xsem.at[g, w])

    def load_tables():
        return [
            pltpu.make_async_copy(pairs_hbm, pairs_ref, tsem.at[0]),
            pltpu.make_async_copy(count_hbm, count_ref, tsem.at[1]),
            pltpu.make_async_copy(first_hbm, first, tsem.at[2]),
            pltpu.make_async_copy(added_hbm, added, tsem.at[3]),
        ]

    rows_copy = pltpu.make_async_copy(rows_hbm, rows_ref, tsem.at[4])
    rows_copy.start()
    for w in range(windows):
        load_x(0, w).start()

    barrier = pltpu.get_barrier_semaphore()

    deep = 8
    wide = owners // deep
    y, z = me // deep, lax.rem(me, deep)

    def owner_at(dy, dz):
        return lax.rem(y + dy, wide) * deep + lax.rem(z + dz, deep)

    def near(i):
        along_y = i // deep
        odd = lax.rem(i, 2)
        dz = odd * ((i + 1) // 2) + (1 - odd) * (deep - i // 2)
        return owner_at(along_y * lax.rem(i + 1, deep), (1 - along_y) * dz)

    def far(i):
        return owner_at(1 + i // (deep - 1), 1 + lax.rem(i, deep - 1))

    def greet_owner(i, _):
        pl.semaphore_signal(barrier, inc=1, device_id=(near(i), tm), device_id_type=MESH)
        return 0

    def greet_time(i, _):
        pl.semaphore_signal(barrier, inc=1, device_id=(me, lax.rem(tm + i, times)), device_id_type=MESH)
        return 0

    lax.fori_loop(1, deep + wide - 1, greet_owner, 0)
    lax.fori_loop(1, times, greet_time, 0)
    for g in range(1, groups):
        for w in range(windows):
            load_x(g, w).start()
    for copy in load_tables():
        copy.start()

    rows_copy.wait()

    def prepare(g):
        for w in range(windows):
            load_x(g, w).wait()

        def one(o, _):
            base = lax.rem(o, 4) * (16 * GROUP)
            for k in range(capacity):
                r = rows_ref[k, o]
                for w in range(windows):
                    v = xbufs[g][r, w * 2 * GROUP : (w + 1) * 2 * GROUP, :]
                    stage[pl.ds(base + k * windows + w, 2 * GROUP, stride=8), :] = v.astype(F32)
            for t in range(GROUP):
                sendbuf[g, o, :, t * LANES : (t + 1) * LANES] = stage[pl.ds(base + t * 16, 16), :].astype(BF16)
            return 0

        lax.fori_loop(0, owners, one, 0, unroll=2)

    def lanes(c):
        g, t0, nt = chunks[c]
        return pl.ds(t0 * LANES, nt * LANES)

    def source(g):
        return latebuf if g == late else sendbuf.at[g]

    def send(c):
        g = chunks[c][0]

        def start(to):
            pltpu.make_async_remote_copy(
                src_ref=source(g).at[to, :, lanes(c)], dst_ref=recvbuf.at[g, me, :, lanes(c)],
                send_sem=ssem.at[c], recv_sem=rsem.at[c], device_id=(to, tm), device_id_type=MESH,
            ).start()

        def one_near(i, _):
            start(near(i))
            return 0

        def one_far(i, _):
            start(far(i))
            return 0

        def pass_on(i, _):
            pl.semaphore_signal(rowsem, inc=1, device_id=(owner_at(i, 0), tm), device_id_type=MESH)
            return 0

        if c == 0:
            lax.fori_loop(1, wide, pass_on, 0)
            lax.fori_loop(1, deep + wide - 1, one_near, 0)
            pl.semaphore_wait(rowsem, wide - 1)
        lax.fori_loop(0, (deep - 1) * (wide - 1), one_far, 0)
        if c:
            lax.fori_loop(1, deep + wide - 1, lambda i, _: one_near(deep + wide - 1 - i, 0), 0)
        pltpu.make_async_copy(source(g).at[me, :, lanes(c)], recvbuf.at[g, me, :, lanes(c)], lsem.at[c]).start()

    def wait_received(c):
        g = chunks[c][0]
        others = recvbuf.at[g, pl.ds(0, owners - 1), :, lanes(c)]
        pltpu.make_async_copy(others, others, rsem.at[c]).wait()
        own = recvbuf.at[g, me, :, lanes(c)]
        pltpu.make_async_copy(own, own, lsem.at[c]).wait()

    def wait_sent(c):
        g = chunks[c][0]
        others = source(g).at[pl.ds(0, owners - 1), :, lanes(c)]
        pltpu.make_async_copy(others, others, ssem.at[c]).wait()

    def tile(t):
        return pl.ds(pl.multiple_of(t * LANES, LANES), LANES)

    own_tile = pltpu.make_async_copy(sendbuf.at[late, :, :, tile(tm)], latebuf.at[:, :, tile(tm)], esem.at[2])

    def trade():
        def one(i, _):
            to = lax.rem(tm + i, times)
            pltpu.make_async_remote_copy(
                src_ref=sendbuf.at[late, :, :, tile(to)], dst_ref=latebuf.at[:, :, tile(tm)],
                send_sem=esem.at[0], recv_sem=esem.at[1], device_id=(me, to), device_id_type=MESH,
            ).start()
            return 0

        lax.fori_loop(1, times, one, 0)
        own_tile.start()

    def wait_traded():
        others = latebuf.at[:, :, pl.ds(0, (times - 1) * LANES)]
        pltpu.make_async_copy(others, others, esem.at[1]).wait()
        own_tile.wait()

        def pack(o, _):
            for row in range(times // 2):
                x = latebuf[o, :, row * 2 * LANES : (row * 2 + 1) * LANES].astype(F32)
                y = latebuf[o, :, (row * 2 + 1) * LANES : (row * 2 + 2) * LANES].astype(F32)
                for h in range(2):
                    cut = slice(h * HALF, (h + 1) * HALF)
                    packed[h * (times // 2) + row] = jnp.concatenate([x[:, cut], y[:, cut]], axis=1).astype(BF16)
            for t in range(times):
                latebuf[o, :, t * LANES : (t + 1) * LANES] = packed[t]
            return 0

        lax.fori_loop(0, owners, pack, 0)

    for g in (0, late, *range(1, late)):
        prepare(g)
        if g == 0:
            pl.semaphore_wait(barrier, deep + wide - 2 + times - 1)
        if g == late:
            trade()
        for c in range(len(chunks)):
            if chunks[c][0] == g < late:
                send(c)

    for copy in load_tables():
        copy.wait()

    lines = 8 * owners
    column = lax.broadcasted_iota(jnp.int32, (npairs, lines), 1)
    slot = lax.broadcasted_iota(jnp.int32, (npairs, lines), 0)
    live = slot < count_ref[0]
    for side in range(2):
        ids = jnp.transpose(jnp.broadcast_to(pairs_ref[side : side + 1, :], (LANES, npairs)))
        line = jnp.concatenate([ids * windows] * (lines // LANES), axis=1)
        for w in range(windows):
            hit = column == line + w
            if side == 0:
                hit = hit & live
            ohot[side, w] = jnp.where(hit, 1.0, 0.0).astype(F32).astype(BF16)

    acc[...] = jnp.zeros(acc.shape, F32)

    def split(value):
        high = value.astype(BF16)
        return high, (value - high.astype(F32)).astype(BF16)

    def make_table(g):
        def one(i, _):
            t, n = i // (LAGS // 256), lax.rem(i, LAGS // 256)
            at = pl.ds(pl.multiple_of(n * 256, 256), 256)
            c0, s0 = first[g * GROUP + t, 0:1, at], first[g * GROUP + t, 1:2, at]
            c1, s1 = added[0, :, at], added[1, :, at]
            for part, value in enumerate((c0 * c1 - s0 * s1, -(s0 * c1 + c0 * s1))):
                for i, piece in enumerate(split(value)):
                    if g == late:
                        for h in range(2):
                            row = h * LANES + part * HALF
                            tbuf[t, i, row : row + HALF, at] = piece[h * HALF : (h + 1) * HALF]
                    else:
                        tbuf[t, i, part * LANES : (part + 1) * LANES, at] = piece
            return 0

        lax.fori_loop(0, GROUP * (LAGS // 256), one, 0)

    def cross(g, at, width):
        both = recvbuf[g, :, :, pl.ds(at, width)].astype(F32)
        rows = [both[:, part * 8 : part * 8 + 8, :].reshape(8 * owners, width).astype(BF16) for part in range(2)]
        rows = jnp.concatenate(rows, axis=1)
        real = None
        for w in range(windows):
            a = jnp.dot(ohot[0, w], rows, preferred_element_type=F32)
            b = jnp.dot(ohot[1, w], rows, preferred_element_type=F32)
            a, b = [(v[:, :width], v[:, width:]) for v in (a, b)]
            re = a[0] * b[0] + a[1] * b[1]
            im = a[1] * b[0] - a[0] * b[1]
            real, imag = (re, im) if real is None else (real + re, imag + im)
        return real, imag

    def early_chunk(g, t0, nt):
        def piece(i, _):
            at = pl.multiple_of((t0 + 2 * i) * LANES, 2 * LANES)
            for part, value in enumerate(cross(g, at, 2 * LANES)):
                high, low = split(value)
                for t in range(2):
                    to = pl.ds(pl.multiple_of((2 * i + t) * 2 * LANES, 2 * LANES) + part * LANES, LANES)
                    dhi[:, to] = high[:, t * LANES : (t + 1) * LANES]
                    dlo[:, to] = low[:, t * LANES : (t + 1) * LANES]
            return 0

        lax.fori_loop(0, nt // 2, piece, 0)
        depth = nt * 2 * LANES

        def lag_tile(n, _):
            at = pl.ds(pl.multiple_of(n * 256, 256), 256)
            thi = tbuf[t0 : t0 + nt, 0, :, at].reshape(depth, 256)
            tlo = tbuf[t0 : t0 + nt, 1, :, at].reshape(depth, 256)
            high = dhi[:, :depth]
            total = jnp.dot(high, thi, preferred_element_type=F32)
            total += jnp.dot(dlo[:, :depth], thi, preferred_element_type=F32)
            total += jnp.dot(high, tlo, preferred_element_type=F32)
            acc[:, at] += total
            return 0

        lax.fori_loop(0, LAGS // 256, lag_tile, 0)

    def late_chunk(t0, nt):
        def piece(i, _):
            at = pl.multiple_of((t0 + 2 * i) * LANES, 2 * LANES)
            for part, value in enumerate(cross(late, at, 2 * LANES)):
                sums[part] += value[:, :LANES] + value[:, LANES:]
            return 0

        if t0 % (times // 2) == 0:
            sums[...] = jnp.zeros(sums.shape, F32)
        if nt > 1:
            lax.fori_loop(0, nt // 2, piece, 0)
        else:
            for part, value in enumerate(cross(late, t0 * LANES, LANES)):
                sums[part] += value

    def finish_half(h):
        halves = [sums[part, :, :HALF] + sums[part, :, HALF:] for part in range(2)]
        stack[h] = jnp.concatenate(halves, axis=1)
        give(stack.at[h], parts.at[h], usem.at[h], vsem.at[h])
        parts[h, tm] = stack[h, block(tm), :]

    def block(t):
        return pl.ds(pl.multiple_of(t * share, 8), share)

    def give(src, dst, send_sem, recv_sem):
        def one(i, _):
            far = lax.rem(i, 2) * (times // 2 + (i - 1) // 2) + (1 - lax.rem(i, 2)) * (times // 2 - i // 2)
            to = lax.rem(tm + far, times)
            pltpu.make_async_remote_copy(
                src_ref=src.at[block(to), :], dst_ref=dst.at[tm], send_sem=send_sem, recv_sem=recv_sem.at[far],
                device_id=(me, to), device_id_type=MESH,
            ).start()
            return 0

        lax.fori_loop(1, times, one, 0)

    def wait_given(src, sem):
        given = src.at[pl.ds(0, (times - 1) * share), :]
        pltpu.make_async_copy(given, given, sem).wait()

    def wait_part(dst, sem, i):
        come = dst.at[lax.rem(tm + times - i, times)]
        pltpu.make_async_copy(come, come, sem.at[i]).wait()

    for c, (g, t0, nt) in enumerate(chunks):
        if t0 == 0:
            make_table(g)
        if c == 1:
            wait_traded()
            for d in range(len(chunks)):
                if chunks[d][0] == late:
                    send(d)
        wait_received(c)
        if g < late:
            early_chunk(g, t0, nt)
            if chunks[c + 1][0] == late:
                give(acc, summed, psem, qsem)
        else:
            late_chunk(t0, nt)
            if (t0 + nt) % (times // 2) == 0:
                finish_half(t0 // (times // 2))

    for i in range(1, times):
        wait_part(summed, qsem, i)
    summed[tm] = acc[block(tm), :]
    total = summed[0]
    for t in range(1, times):
        total = total + summed[t]
    out_ref[...] = total

    def shift(j):
        odd = lax.rem(j, 2)
        return odd * ((j + 1) // 2) + (1 - odd) * lax.rem(times - j // 2, times)

    for h in range(2):

        def lag_part(step, _):
            high, low, thi, tlo = [], [], [], []
            for side in range(2):
                i = shift(2 * step + side)
                if side:
                    wait_part(parts.at[h], vsem.at[h], i)
                else:

                    @pl.when(step > 0)
                    def _():
                        wait_part(parts.at[h], vsem.at[h], i)

                t = lax.rem(tm + times - i, times)
                for part, into in zip(split(parts[h, t]), (high, low)):
                    into.append(part)
                thi.append(tbuf[t, 0, h * LANES : (h + 1) * LANES])
                tlo.append(tbuf[t, 1, h * LANES : (h + 1) * LANES])
            high, low = jnp.concatenate(high, axis=1), jnp.concatenate(low, axis=1)
            value = jnp.dot(jnp.concatenate([high, low]), jnp.concatenate(thi), preferred_element_type=F32)
            value = value[:share] + value[share:] + jnp.dot(high, jnp.concatenate(tlo), preferred_element_type=F32)
            out_ref[...] += value
            return 0

        lax.fori_loop(0, times // 2, lag_part, 0)
    out_ref[...] *= scale
    wait_given(acc, psem)
    for h in range(2):
        wait_given(stack.at[h], usem.at[h])
    others = sendbuf.at[late, :, :, pl.ds(0, (times - 1) * LANES)]
    pltpu.make_async_copy(others, others, esem.at[0]).wait()
    for c in range(len(chunks)):
        wait_sent(c)


def shards(first, added, spectra, send_rows, pair_list, pair_count):
    owners = lax.axis_size("pair")
    times = lax.axis_size("tm")
    channels, windows, _, bins = spectra.shape
    capacity = send_rows.shape[2]
    npairs = pair_list.shape[1]
    tiles = bins // LANES
    groups = tiles // GROUP
    lines = spectra.reshape(channels, windows, 2, tiles, LANES).transpose(0, 1, 3, 2, 4)
    lines = lines.reshape(channels, windows * tiles * 2, LANES)
    last = groups - 1
    chunks = [(g, 0, GROUP) for g in range(last - 1)]
    chunks += [(last - 1, a, b) for a, b in [(0, 4), (4, 4)]]
    chunks += [(last, a, b) for a, b in [(0, 4), (4, 2), (6, 2)]]
    scale = (2.0 * bins * windows * times) ** (-0.5)
    dims = (owners, times, capacity, windows, groups, npairs, tuple(chunks), scale)
    rows = jnp.transpose(send_rows, (0, 2, 1)).reshape(capacity, owners)
    nc = len(chunks)
    dma = pltpu.SemaphoreType.DMA
    return pl.pallas_call(
        functools.partial(kernel, dims),
        out_shape=pltpu.VMEM((npairs // times, LAGS), F32),
        in_specs=[pl.BlockSpec(memory_space=pltpu.HBM)] * 6,
        out_specs=pl.BlockSpec(memory_space=pltpu.VMEM),
        scratch_shapes=[
            *[pltpu.VMEM((channels, windows * 2 * GROUP, LANES), BF16)] * groups,
            pltpu.SMEM(rows.shape, jnp.int32),
            pltpu.VMEM(pair_list.shape, jnp.int32),
            pltpu.SMEM((1,), jnp.int32),
            pltpu.VMEM((4 * 16 * GROUP, LANES), F32),
            pltpu.VMEM((groups, owners, 16, GROUP * LANES), BF16),
            pltpu.VMEM((owners, 16, GROUP * LANES), BF16),
            pltpu.VMEM((groups, owners, 16, GROUP * LANES), BF16),
            pltpu.VMEM((2, windows, npairs, 8 * owners), BF16),
            pltpu.VMEM((npairs, GROUP * 2 * LANES), BF16),
            pltpu.VMEM((npairs, GROUP * 2 * LANES), BF16),
            pltpu.VMEM((GROUP, 2, 2 * LANES, LAGS), BF16),
            pltpu.VMEM(first.shape, F32),
            pltpu.VMEM(added.shape, F32),
            pltpu.VMEM((npairs, LAGS), F32),
            pltpu.VMEM((times, npairs // times, LAGS), F32),
            pltpu.VMEM((2, npairs, LANES), F32),
            pltpu.VMEM((2, npairs, LANES), F32),
            pltpu.VMEM((2, times, npairs // times, LANES), F32),
            pltpu.VMEM((times, 16, LANES), BF16),
            dma((groups, windows)),
            dma((5,)),
            dma((nc,)),
            dma((nc,)),
            dma((nc,)),
            dma((3,)),
            dma,
            dma((times,)),
            dma((2,)),
            dma((2, times)),
            pltpu.SemaphoreType.REGULAR,
        ],
        compiler_params=pltpu.CompilerParams(
            collective_id=0, has_side_effects=True, vmem_limit_bytes=58 * 1024 * 1024
        ),
        name="correlate",
    )(lines, rows, pair_list, pair_count, first, added)


def solution(mesh):
    first, added = lag_tables(4096, LAGS)

    def run(spectra, send_rows, pair_list, pair_count):
        in_specs = (P(), P(), P("pair", "tm", None, None), P("pair", None, None), P(None, "pair"), P("pair"))
        body = jax.shard_map(
            shards, mesh=mesh, in_specs=in_specs, out_specs=P(("pair", "tm"), None), check_vma=False
        )
        return body(jnp.asarray(first), jnp.asarray(added), spectra, send_rows, pair_list, pair_count)

    return run
```
